128 devices in a mesh: gx: 8 (over x, y_hi), gy: 16 (over z, y_lo, core).
Axes of the slice: x: 4, y: 4 (y_hi: 2, y_lo: 2; y = y_hi * 2 + y_lo), z: 4, core: 2. Of those that a mesh axis runs over, the one named last changes fastest.
Arguments:
- child_state: float32 [4, 8, 2048, 2048], P(None, None, 'gx', 'gy'), may hold values from -6 to 6
- parent_slab: float32 [4, 8, 2048, 128], P(None, None, ('gx', 'gy')), may hold values from -6 to 6
- parent_above: float32 [4, 2048, 128], P(None, ('gx', 'gy')), may hold values from -6 to 6
- radiative_mean_kelvin: float32 [2048, 2048], P('gx', 'gy'), may hold values from -6 to 6
- courant_x: float32 [8], replicated, may hold values from -0.8 to 0.8
- courant_y: float32 [8], replicated, may hold values from -0.8 to 0.8
- diffusion: float32 [4], replicated, may hold values from 0.05 to 0.15
- building: int32 [8, 2048, 2048], P(None, 'gx', 'gy'), may hold values 0 or 1
- fine_tile: int32 [2048, 16], P(('gx', 'gy')), may hold values from 0 to 3
- fine_row: int32 [2048, 16], P(('gx', 'gy')), may hold values from 0 to 255
- fine_op: int32 [2048, 16], P(('gx', 'gy')), may hold values from 0 to 7
- fine_bank: float32 [8, 128, 128], replicated, may hold values from -0.125 to 0.125
- coarse_tile: int32 [2048, 16, 4], P('gx', 'gy'), may hold values from 0 to 3
- coarse_row: int32 [2048, 16, 4], P('gx', 'gy'), may hold values from 0 to 15
- coarse_op: int32 [2048, 16, 4], P('gx', 'gy'), may hold values from 0 to 7
- coarse_bank: float32 [8, 128, 128], replicated, may hold values from -0.25 to 0.25
Outputs:
- nested_domain_states: float32 [4, 8, 2048, 2048], P(None, None, 'gx', 'gy')
- parent_new: float32 [4, 8, 2048, 128], P(None, None, ('gx', 'gy'))
- comfort: float32 [2048, 2048], P('gx', 'gy')
The draws below stay inside these ranges and needn't reach their ends.
All inputs are finite; a program needn't handle non-finite values. No bound on the sum of `building` on one device may be relied on, other than what follows from the above.
Results may differ from the reference program's by a relative error of at most 0.0003.
Values sent between devices are 32-bit elements; how exact they have to be, the bound alone decides.
No kernel may reach another device: no remote copies, remote signals or barrier semaphores. Data moves between devices by JAX's collectives and lax.ppermute only.
A program may use at most 128 MiB of HBM per device.

```python
import jax
import jax.numpy as jnp
from jax import lax

V = 4
NZ = 8
BLK = 128
CX = 256
K = 16
KI = 4
NOPS = 8
PB = 16
NXC = 2048
NYC = 2048
NPB = 2048
N_GX = 8
N_GY = 16


def place_ends(drawn, rng, low, top_value):
    shape = drawn.shape
    place = [jax.random.randint(jax.random.fold_in(rng, axis), (), 0, shape[axis]) for axis in range(len(shape))]
    drawn = drawn.at[tuple(place)].set(low)
    longest = shape.index(max(shape))
    place[longest] = (place[longest] + 1) % shape[longest]
    return drawn.at[tuple(place)].set(top_value)


def level_of(key, dims, pieces, least, high):
    gain, own = 1.0, jax.random.fold_in(key, 6)
    for position, shards_of in pieces:
        draws = jnp.exp(jax.random.uniform(jax.random.fold_in(own, position), (shards_of,), jnp.float32, least / len(pieces), high / len(pieces)))
        gain = gain * jnp.repeat(draws, dims[position] // shards_of).reshape([-1 if axis == position else 1 for axis in range(len(dims))])
    return gain


def gaussian(rng, extent, deviation, reach, cuts=(), kind=jnp.bfloat16):
    values = deviation * jax.random.normal(rng, extent, jnp.float32)
    if cuts:
        values = values * level_of(rng, extent, cuts, -0.22, 0.18)
    return jnp.clip(values, -reach, reach).astype(kind)


def setup_inputs(seed: int = 0) -> dict:
    key_list = jax.random.split(jax.random.key(seed), 17)
    child_state = gaussian(key_list[0], (V, NZ, NXC, NYC), 1.0, 6.0, ((2, 8), (3, 16)), jnp.float32)
    parent_slab = gaussian(key_list[1], (V, NZ, NPB, BLK), 1.0, 6.0, ((2, 128),), jnp.float32)
    parent_above = gaussian(key_list[2], (V, NPB, BLK), 1.0, 6.0, ((1, 128),), jnp.float32)
    radiative_mean_kelvin = gaussian(key_list[3], (NXC, NYC), 1.0, 6.0, ((0, 8), (1, 16)), jnp.float32)
    courant_x = jnp.clip(jax.random.uniform(key_list[4], (NZ,), jnp.float32, -0.8, 0.8), -0.8, 0.8)
    courant_y = jnp.clip(jax.random.uniform(key_list[5], (NZ,), jnp.float32, -0.8, 0.8), -0.8, 0.8)
    diffusion = jnp.clip(jax.random.uniform(key_list[6], (V,), jnp.float32, 0.05, 0.15), 0.05, 0.15)
    building = place_ends((jax.random.randint(key_list[7], (NZ, NXC, NYC), 0, 4) < 1).astype(jnp.int32), jax.random.fold_in(key_list[7], 1), 0, 1)
    fine_tile = place_ends(jax.random.randint(key_list[8], (NPB, K), 0, 4), jax.random.fold_in(key_list[8], 1), 0, 3).astype(jnp.int32)
    fine_row = place_ends(jax.random.randint(key_list[9], (NPB, K), 0, CX), jax.random.fold_in(key_list[9], 1), 0, CX - 1).astype(jnp.int32)
    fine_op = place_ends(jax.random.randint(key_list[10], (NPB, K), 0, NOPS), jax.random.fold_in(key_list[10], 1), 0, NOPS - 1).astype(jnp.int32)
    fine_bank = gaussian(key_list[11], (NOPS, BLK, BLK), (BLK * K) ** -0.5, 0.125, (), jnp.float32)
    coarse_tile = place_ends(jax.random.randint(key_list[12], (NXC, N_GY, KI), 0, 4), jax.random.fold_in(key_list[12], 1), 0, 3).astype(jnp.int32)
    coarse_row = place_ends(jax.random.randint(key_list[13], (NXC, N_GY, KI), 0, PB), jax.random.fold_in(key_list[13], 1), 0, PB - 1).astype(jnp.int32)
    coarse_op = place_ends(jax.random.randint(key_list[14], (NXC, N_GY, KI), 0, NOPS), jax.random.fold_in(key_list[14], 1), 0, NOPS - 1).astype(jnp.int32)
    coarse_bank = gaussian(key_list[15], (NOPS, BLK, BLK), (BLK * KI) ** -0.5, 0.25, (), jnp.float32)
    return {"child_state": child_state, "parent_slab": parent_slab, "parent_above": parent_above, "radiative_mean_kelvin": radiative_mean_kelvin, "courant_x": courant_x, "courant_y": courant_y, "diffusion": diffusion, "building": building, "fine_tile": fine_tile, "fine_row": fine_row, "fine_op": fine_op, "fine_bank": fine_bank, "coarse_tile": coarse_tile, "coarse_row": coarse_row, "coarse_op": coarse_op, "coarse_bank": coarse_bank}


precise_setting = lax.Precision.HIGHEST
relaxation = 0.5

def beam_warming(centre, near_low, far_low, near_high, distant_upper, courant):
    magnitude = jnp.abs(courant)
    from_low = -0.5 * magnitude * (3.0 * centre - 4.0 * near_low + far_low) + 0.5 * magnitude * magnitude * (centre - 2.0 * near_low + far_low)
    from_high = -0.5 * magnitude * (3.0 * centre - 4.0 * near_high + distant_upper) + 0.5 * magnitude * magnitude * (centre - 2.0 * near_high + distant_upper)
    return jnp.where(courant >= 0.0, from_low, from_high)

def advance(padded, top_ghost, courant_x, courant_y, diffusion, building):
    centre = padded[:, :, 2:-2, 2:-2]
    west_near = padded[:, :, 1:-3, 2:-2]
    west_far = padded[:, :, :-4, 2:-2]
    east_near = padded[:, :, 3:-1, 2:-2]
    east_far = padded[:, :, 4:, 2:-2]
    south_near = padded[:, :, 2:-2, 1:-3]
    south_far = padded[:, :, 2:-2, :-4]
    north_near = padded[:, :, 2:-2, 3:-1]
    north_far = padded[:, :, 2:-2, 4:]
    along_x = beam_warming(centre, west_near, west_far, east_near, east_far, courant_x[None, :, None, None])
    along_y = beam_warming(centre, south_near, south_far, north_near, north_far, courant_y[None, :, None, None])
    beneath = jnp.concatenate([jnp.zeros_like(centre[:, :1]), centre[:, :-1]], axis=1)
    overhead = jnp.concatenate([centre[:, 1:], top_ghost[:, None]], axis=1)
    laplace = west_near + east_near + south_near + north_near + beneath + overhead - 6.0 * centre
    stepped = centre + along_x + along_y + diffusion[:, None, None, None] * laplace
    return jnp.where(building[None] == 1, 0.0, stepped)

def comfort_index(nested_domain_states, radiative_mean_kelvin):
    wind_u = nested_domain_states[0, 0]
    wind_v = nested_domain_states[1, 0]
    ambient_kelvin = nested_domain_states[2, 0]
    moisture_ratio = nested_domain_states[3, 0]
    flow_speed_norm = jnp.sqrt(wind_u * wind_u + wind_v * wind_v + 0.25)
    excess_quantity = radiative_mean_kelvin - ambient_kelvin
    return ambient_kelvin + 0.3 * excess_quantity - 0.6 * (flow_speed_norm - 1.0) + 0.4 * moisture_ratio + 0.1 * ambient_kelvin * excess_quantity - 0.15 * flow_speed_norm * excess_quantity

def step_after(tiles, axis):
    length = tiles.shape[axis]
    return jnp.concatenate([lax.slice_in_dim(tiles, 1, length, axis=axis), jnp.zeros_like(lax.slice_in_dim(tiles, 0, 1, axis=axis))], axis=axis)

def step_before(tiles, axis):
    length = tiles.shape[axis]
    return jnp.concatenate([jnp.zeros_like(lax.slice_in_dim(tiles, 0, 1, axis=axis)), lax.slice_in_dim(tiles, 0, length - 1, axis=axis)], axis=axis)

def reference(child_state, parent_slab, parent_above, radiative_mean_kelvin, courant_x, courant_y, diffusion, building, fine_tile, fine_row, fine_op, fine_bank, coarse_tile, coarse_row, coarse_op, coarse_bank):
    index_x = jnp.arange(N_GX, dtype=jnp.int32)
    index_y = jnp.arange(N_GY, dtype=jnp.int32)
    parent_tiles = parent_above.reshape(V, N_GX, N_GY, PB, BLK)
    parent_west = step_before(parent_tiles, 1)
    parent_sources = jnp.stack([parent_tiles, parent_west, step_before(parent_tiles, 2), step_before(parent_west, 2)])
    tile_ids = coarse_tile.reshape(N_GX, CX, N_GY, KI)
    row_ids = coarse_row.reshape(N_GX, CX, N_GY, KI)
    op_ids = coarse_op.reshape(N_GX, CX, N_GY, KI)
    picked = parent_sources[tile_ids, :, index_x[:, None, None, None], index_y[None, None, :, None], row_ids, :]
    top_ghost = jnp.zeros((V, N_GX, CX, N_GY, BLK), jnp.float32)
    for operator_position in range(NOPS):
        chosen = (op_ids == operator_position).astype(jnp.float32)
        combined_fields = jnp.einsum('xayk,xaykvb->vxayb', chosen, picked, precision=precise_setting)
        top_ghost = top_ghost + jnp.einsum('cb,vxayb->vxayc', coarse_bank[operator_position], combined_fields, precision=precise_setting)
    top_ghost = top_ghost.reshape(V, N_GX * CX, N_GY * BLK)
    padded = jnp.pad(child_state, ((0, 0), (0, 0), (2, 2), (2, 2)))
    nested_domain_states = advance(padded, top_ghost, courant_x, courant_y, diffusion, building)
    child_tiles = nested_domain_states.reshape(V, NZ, N_GX, CX, N_GY, BLK)
    shifted = step_after(child_tiles, 2)
    child_sources = jnp.stack([child_tiles, shifted, step_after(child_tiles, 4), step_after(shifted, 4)])
    tile_ids = fine_tile.reshape(N_GX, N_GY, PB, K)
    row_ids = fine_row.reshape(N_GX, N_GY, PB, K)
    op_ids = fine_op.reshape(N_GX, N_GY, PB, K)
    picked = child_sources[tile_ids, :, :, index_x[:, None, None, None], row_ids, index_y[None, :, None, None], :]
    anterp = jnp.zeros((V, NZ, N_GX, N_GY, PB, BLK), jnp.float32)
    for operator_position in range(NOPS):
        chosen = (op_ids == operator_position).astype(jnp.float32)
        combined_fields = jnp.einsum('ijpk,ijpkvzb->vzijpb', chosen, picked, precision=precise_setting)
        anterp = anterp + jnp.einsum('cb,vzijpb->vzijpc', fine_bank[operator_position], combined_fields, precision=precise_setting)
    anterp = anterp.reshape(V, NZ, N_GX * N_GY * PB, BLK)
    parent_new = (1.0 - relaxation) * parent_slab + relaxation * anterp
    return (nested_domain_states, parent_new, comfort_index(nested_domain_states, radiative_mean_kelvin))
```

```python
import jax
import jax.numpy as jnp
from jax import lax
from jax.experimental import pallas as pl
from jax.experimental.pallas import tpu as pltpu
from jax.sharding import PartitionSpec as P

V, NZ, BLK, CX, K, KI, NOPS, PB = 4, 8, 128, 256, 16, 4, 8, 16
VZ = V * NZ
F32, BF16 = jnp.float32, jnp.bfloat16
PAD = 8
CHUNK = 64
VMEM_BYTES = 48 * 1024 * 1024

X_ROWS, X_PAR, X_IDX, X_ALL = 0, 64, 128, 144
Y_COLS, Y_PAR, Y_RELAY, Y_IDX, Y_RIDX, Y_ALL = 0, 128, 192, 256, 272, 288

ANY = pl.BlockSpec(memory_space=pl.ANY)
IN_VMEM = pl.BlockSpec(memory_space=pltpu.VMEM)
IN_SMEM = pl.BlockSpec(memory_space=pltpu.SMEM)
NT = (((1,), (1,)), ((), ()))
TN = (((0,), (0,)), ((), ()))


def exchange(value, axis, odd):
    pairs = []
    for a in range(odd, lax.axis_size(axis) - 1, 2):
        pairs += [(a, a + 1), (a + 1, a)]
    return lax.ppermute(value, axis, pairs)


def one_lower(value, axis):
    return lax.ppermute(value, axis, [(a, a - 1) for a in range(1, lax.axis_size(axis))])


def split(value):
    high = value.astype(BF16)
    return high, (value - high.astype(F32)).astype(BF16)


def lanes(shape):
    return lax.broadcasted_iota(jnp.int32, shape, len(shape) - 1)


def pack_kernel(parity, child, parent, tile, row, op, even, odd, to_next, to_prev, cells, stage, sems):
    copies = [pltpu.make_async_copy(child.at[pl.ds(NZ * v, NZ)], cells.at[pl.ds(NZ * v, NZ)], sems.at[v]) for v in range(V)]
    for c in copies:
        c.start()
    stage[...] = jnp.zeros_like(stage)
    stage[0, :, 0:K] = tile[...].astype(F32)
    stage[1, :, 0:K] = row[...].astype(F32)
    stage[2, :, 0:K] = op[...].astype(F32)
    index = stage[0] + pltpu.roll(stage[1], K, 1) + pltpu.roll(stage[2], 2 * K, 1)
    flag = parity[0] == 0
    for buffer in (even, odd):
        buffer[X_PAR:X_IDX] = parent[...]
        buffer[X_IDX:X_ALL] = index
    which = lanes((CX, BLK)) // 4
    edges = jnp.zeros((CX, BLK), F32)
    for v in range(V):
        copies[v].wait()
        for z in range(NZ):
            vz = NZ * v + z
            low, high = cells[vz, 0:2], cells[vz, CX - 2 : CX]
            even[2 * vz : 2 * vz + 2] = jnp.where(flag, high, low)
            odd[2 * vz : 2 * vz + 2] = jnp.where(flag, low, high)
            edges = jnp.where(which == vz, pltpu.roll(cells[vz], (4 * vz + 2) % BLK, 1), edges)
    half = CX // 2
    upper = lanes((half, BLK)) % 4 >= 2
    to_next[...] = jnp.where(upper, pltpu.roll(edges[half:], 2, 1), edges[:half])
    to_prev[...] = jnp.where(upper, edges[:half], pltpu.roll(edges[half:], BLK - 2, 1))


def join_kernel(parity, even_x, odd_x, own_even, to_next, to_prev, even, odd):
    flag_x, flag = parity[0] == 0, parity[1] == 0
    even[Y_COLS:Y_PAR] = jnp.where(flag, to_next[...], to_prev[...])
    odd[Y_COLS:Y_PAR] = jnp.where(flag, to_prev[...], to_next[...])
    relay = jnp.where(flag_x, odd_x[X_PAR:X_ALL], even_x[X_PAR:X_ALL])
    own = own_even[X_PAR:X_ALL]
    for buffer in (even, odd):
        buffer[Y_PAR:Y_RELAY] = own[:64]
        buffer[Y_RELAY:Y_IDX] = relay[:64]
        buffer[Y_IDX:Y_RIDX] = own[64:]
        buffer[Y_RIDX:Y_ALL] = relay[64:]


def main_kernel(
    parity, courant_x, courant_y, diffusion,
    child, building, own_x, even_x, odd_x, even_y, odd_y, fine_bank, coarse_bank, coarse_code, radiant,
    states, comfort, part_own, part_x, part_y,
    cells, new, walls, ground, halo, select, banks, ghost, table, fields, picked_high, picked_low, sems, out_sems,
):
    flag_x, flag_y = parity[0] == 0, parity[1] == 0
    walls_in = pltpu.make_async_copy(building, walls, sems.at[V])
    copies = [
        pltpu.make_async_copy(child.at[pl.ds(NZ * v, NZ)], cells.at[v, :, pl.ds(PAD, CX)], sems.at[v]) for v in range(V)
    ]
    copies[0].start()
    walls_in.start()
    for c in copies[1:]:
        c.start()

    prev_x = jnp.where(flag_x, odd_x[...], even_x[...])
    prev_y = jnp.where(flag_y, odd_y[...], even_y[...])
    parents = [own_x[X_PAR:X_IDX], prev_x[X_PAR:X_IDX], prev_y[Y_PAR:Y_RELAY], prev_y[Y_RELAY:Y_IDX]]
    indices = [own_x[X_IDX:X_ALL], prev_x[X_IDX:X_ALL], prev_y[Y_IDX:Y_RIDX], prev_y[Y_RIDX:Y_ALL]]

    next_x = jnp.where(flag_x, even_x[X_ROWS:X_PAR], odd_x[X_ROWS:X_PAR])
    for v in range(V):
        for z in range(NZ):
            vz = NZ * v + z
            cells[v, z, PAD - 2 : PAD] = prev_x[2 * vz : 2 * vz + 2]
            cells[v, z, PAD + CX : PAD + CX + 2] = next_x[2 * vz : 2 * vz + 2]
    half = CX // 2
    next_y = jnp.where(flag_y, even_y[Y_COLS:Y_PAR], odd_y[Y_COLS:Y_PAR])
    before = prev_y[Y_COLS:Y_PAR]
    upper = lanes((half, BLK)) % 4 >= 2
    halo[0:half] = jnp.where(upper, next_y, before)
    halo[half:CX] = jnp.where(upper, pltpu.roll(next_y, 2, 1), pltpu.roll(before, BLK - 2, 1))

    for o in range(NOPS):
        high, low = split(fine_bank[o])
        banks[0:BLK, BLK * o : BLK * (o + 1)] = high
        banks[BLK : 2 * BLK, BLK * o : BLK * (o + 1)] = low

    high, low = split(jnp.concatenate([parents[t][PB * v : PB * (v + 1)] for v in range(V) for t in range(4)], axis=0))
    for o in range(NOPS):
        bank_high, bank_low = split(coarse_bank[o])
        made = (
            lax.dot_general(high, bank_high, NT, preferred_element_type=F32)
            + lax.dot_general(high, bank_low, NT, preferred_element_type=F32)
            + lax.dot_general(low, bank_high, NT, preferred_element_type=F32)
        )
        made_high, made_low = split(made)
        for v in range(V):
            table[64 * o : 64 * (o + 1), BLK * v : BLK * (v + 1)] = made_high[64 * v : 64 * (v + 1)]
            table[512 + 64 * o : 512 + 64 * (o + 1), BLK * v : BLK * (v + 1)] = made_low[64 * v : 64 * (v + 1)]
    wanted = lax.broadcasted_iota(jnp.int32, (512, CX), 0)
    counts = jnp.zeros((512, CX), F32)
    for k in range(KI):
        counts = counts + jnp.where(coarse_code[k : k + 1, :] == wanted, 1.0, 0.0)
    counts = counts.T.astype(BF16)
    ghost[...] = jnp.dot(counts, table[0:512], preferred_element_type=F32) + jnp.dot(
        counts, table[512:1024], preferred_element_type=F32
    )

    codes = []
    for t in range(4):
        names = indices[t]
        rows = pltpu.roll(names, BLK - K, 1)
        ops = pltpu.roll(names, BLK - 2 * K, 1)
        codes.append(jnp.where(names == float(t), ops * float(CX) + rows, -1.0))
    codes = jnp.concatenate(codes, axis=0)
    spread = [jnp.broadcast_to(codes[:, k : k + 1], (64, CX)) for k in range(K)]
    place = lanes((64, CX)).astype(F32)
    for o in range(NOPS):
        total = jnp.zeros((64, CX), F32)
        for k in range(K):
            total = total + jnp.where(spread[k] == place + float(CX * o), 1.0, 0.0)
        total = total.astype(BF16)
        select[64 * o : 64 * (o + 1), 0:CX] = total
        select[64 * o : 64 * (o + 1), CX : 2 * CX] = total

    walls_in.wait()
    lane = lanes((CHUNK, BLK))

    def variable(v, carry):
        pltpu.make_async_copy(child.at[pl.ds(NZ * v, NZ)], cells.at[v, :, pl.ds(PAD, CX)], sems.at[v]).wait()
        d = diffusion[v]
        for z in range(NZ):
            sx, sy = courant_x[z], courant_y[z]
            mx, my = jnp.abs(sx), jnp.abs(sy)
            up_x, up_y = sx >= 0.0, sy >= 0.0
            near_x, near_y = 2.0 * mx - mx * mx, 2.0 * my - my * my
            far_x, far_y = 0.5 * mx * mx - 0.5 * mx, 0.5 * my * my - 0.5 * my
            own = 1.0 + (0.5 * mx * mx - 1.5 * mx) + (0.5 * my * my - 1.5 * my) - 6.0 * d
            low_x = d + jnp.where(up_x, near_x, 0.0)
            high_x = d + jnp.where(up_x, 0.0, near_x)
            low_y = d + jnp.where(up_y, near_y, 0.0)
            high_y = d + jnp.where(up_y, 0.0, near_y)
            low_far = jnp.where(up_x, far_x, 0.0)
            high_far = jnp.where(up_x, 0.0, far_x)
            first_far = jnp.where(up_y, BLK - 2, 0)
            turn_far = jnp.where(up_y, 2, BLK - 2)
            turn = BLK - 2 - (4 * (NZ * v + z)) % BLK
            turn = jnp.where(turn < 0, turn + BLK, turn)
            outside = (lane >= first_far) & (lane < first_far + 2)
            for r in range(0, CX, CHUNK):
                c = cells[v, z, PAD + r : PAD + r + CHUNK]
                edge = pltpu.roll(halo[r : r + CHUNK], turn, 1)
                total = own * c
                total = total + low_x * cells[v, z, PAD + r - 1 : PAD + r - 1 + CHUNK]
                total = total + high_x * cells[v, z, PAD + r + 1 : PAD + r + 1 + CHUNK]
                total = total + low_far * cells[v, z, PAD + r - 2 : PAD + r - 2 + CHUNK]
                total = total + high_far * cells[v, z, PAD + r + 2 : PAD + r + 2 + CHUNK]
                total = total + low_y * pltpu.roll(jnp.where(lane == BLK - 1, edge, c), 1, 1)
                total = total + high_y * pltpu.roll(jnp.where(lane == 0, edge, c), BLK - 1, 1)
                total = total + far_y * pltpu.roll(jnp.where(outside, edge, c), turn_far, 1)
                above = (
                    cells[v, z + 1, PAD + r : PAD + r + CHUNK]
                    if z < NZ - 1
                    else ghost[r : r + CHUNK, pl.ds(pl.multiple_of(BLK * v, BLK), BLK)]
                )
                if z > 0:
                    above = above + cells[v, z - 1, PAD + r : PAD + r + CHUNK]
                total = total + d * above
                total = jnp.where(walls[z, r : r + CHUNK] == 1, 0.0, total)
                new[v, z, r : r + CHUNK] = total
                high, low = split(total)
                fields[r : r + CHUNK, BLK * z : BLK * (z + 1)] = high
                fields[CX + r : CX + r + CHUNK, BLK * z : BLK * (z + 1)] = low
                if z == 0:
                    ground[v, r : r + CHUNK] = total
        pltpu.make_async_copy(new.at[v], states.at[pl.ds(NZ * v, NZ)], out_sems.at[v]).start()
        for z in range(0, NZ, 2):
            found = jnp.dot(select[...], fields[:, BLK * z : BLK * (z + 2)], preferred_element_type=F32)
            high, low = split(found)
            for o in range(NOPS):
                for e in range(2):
                    to = (slice(64 * (z + e), 64 * (z + e + 1)), slice(BLK * o, BLK * (o + 1)))
                    at = (slice(64 * o, 64 * (o + 1)), slice(BLK * e, BLK * (e + 1)))
                    picked_high[to] = high[at]
                    picked_low[to] = low[at]
        first = lax.dot_general(picked_high[...], banks[...], NT, preferred_element_type=F32)
        second = lax.dot_general(picked_low[...], banks[0:BLK], NT, preferred_element_type=F32)
        result = first[:, :BLK] + first[:, BLK:] + second
        for z in range(NZ):
            at = pl.ds(pl.multiple_of(PB * (NZ * v + z), PB), PB)
            part_own[at] = result[64 * z : 64 * z + 16]
            part_x[at] = result[64 * z + 16 : 64 * z + 32]
            part_y[0, at] = result[64 * z + 32 : 64 * z + 48]
            part_y[1, at] = result[64 * z + 48 : 64 * z + 64]
        return carry

    lax.fori_loop(0, V, variable, 0)

    for r in range(0, CX, CHUNK):
        u, w, t, h = (ground[v, r : r + CHUNK] for v in range(V))
        speed = jnp.sqrt(u * u + w * w + 0.25)
        excess = radiant[r : r + CHUNK] - t
        comfort[r : r + CHUNK] = (
            t + 0.3 * excess - 0.6 * (speed - 1.0) + 0.4 * h + 0.1 * t * excess - 0.15 * speed * excess
        )
    for v in range(V):
        pltpu.make_async_copy(new.at[v], states.at[pl.ds(NZ * v, NZ)], out_sems.at[v]).wait()


def shape(*dims):
    return jax.ShapeDtypeStruct(dims, F32)


def local(
    child_state, parent_slab, parent_above, radiative_mean_kelvin, courant_x, courant_y, diffusion, building,
    fine_tile, fine_row, fine_op, fine_bank, coarse_tile, coarse_row, coarse_op, coarse_bank,
):
    parity = jnp.stack([lax.axis_index("gx") % 2, lax.axis_index("gy") % 2]).astype(jnp.int32)
    child = child_state.reshape(VZ, CX, BLK)
    parent = parent_above.reshape(V * PB, BLK)
    params = pltpu.CompilerParams(vmem_limit_bytes=VMEM_BYTES)
    x_even, x_odd, to_next, to_prev = pl.pallas_call(
        pack_kernel,
        out_shape=(shape(X_ALL, BLK), shape(X_ALL, BLK), shape(CX // 2, BLK), shape(CX // 2, BLK)),
        in_specs=[IN_SMEM, ANY] + [IN_VMEM] * 4,
        out_specs=(IN_VMEM,) * 4,
        scratch_shapes=[
            pltpu.VMEM((VZ, CX, BLK), F32), pltpu.VMEM((3, PB, BLK), F32), pltpu.SemaphoreType.DMA((V,)),
        ],
        compiler_params=params,
    )(parity, child, parent, fine_tile, fine_row, fine_op)
    got_x_even = exchange(x_even, "gx", 0)
    got_x_odd = exchange(x_odd, "gx", 1)
    y_even, y_odd = pl.pallas_call(
        join_kernel,
        out_shape=(shape(Y_ALL, BLK), shape(Y_ALL, BLK)),
        in_specs=[IN_SMEM] + [IN_VMEM] * 5,
        out_specs=(IN_VMEM,) * 2,
        compiler_params=params,
    )(parity, got_x_even, got_x_odd, x_even, to_next, to_prev)
    got_y_odd = exchange(y_odd, "gy", 1)
    got_y_even = exchange(y_even, "gy", 0)
    coarse_code = (coarse_op * 64 + coarse_tile * PB + coarse_row).reshape(CX, KI).T
    states, comfort, part_own, part_x, part_y = pl.pallas_call(
        main_kernel,
        out_shape=(
            shape(VZ, CX, BLK), shape(CX, BLK), shape(VZ * PB, BLK), shape(VZ * PB, BLK), shape(2, VZ * PB, BLK),
        ),
        in_specs=[IN_SMEM] * 4 + [ANY] * 2 + [IN_VMEM] * 9,
        out_specs=(ANY,) + (IN_VMEM,) * 4,
        scratch_shapes=[
            pltpu.VMEM((V, NZ, CX + 2 * PAD, BLK), F32),
            pltpu.VMEM((V, NZ, CX, BLK), F32),
            pltpu.VMEM((NZ, CX, BLK), jnp.int32),
            pltpu.VMEM((V, CX, BLK), F32),
            pltpu.VMEM((CX, BLK), F32),
            pltpu.VMEM((512, 2 * CX), BF16),
            pltpu.VMEM((2 * BLK, NOPS * BLK), BF16),
            pltpu.VMEM((CX, V * BLK), F32),
            pltpu.VMEM((1024, V * BLK), BF16),
            pltpu.VMEM((2 * CX, NZ * BLK), BF16),
            pltpu.VMEM((512, NOPS * BLK), BF16),
            pltpu.VMEM((512, NOPS * BLK), BF16),
            pltpu.SemaphoreType.DMA((V + 1,)),
            pltpu.SemaphoreType.DMA((V,)),
        ],
        compiler_params=params,
    )(
        parity, courant_x, courant_y, diffusion,
        child, building, x_even, got_x_even, got_x_odd, got_y_even, got_y_odd, fine_bank, coarse_bank, coarse_code,
        radiative_mean_kelvin,
    )
    got_y = one_lower(part_y, "gy")
    got_x = one_lower(part_x + got_y[1], "gx")
    parent_new = 0.5 * parent_slab.reshape(VZ * PB, BLK) + 0.5 * ((part_own + got_y[0]) + got_x)
    return states.reshape(child_state.shape), parent_new.reshape(parent_slab.shape), comfort


def solution(mesh):
    placed = (
        P(None, None, "gx", "gy"),
        P(None, None, ("gx", "gy"), None),
        P(None, ("gx", "gy"), None),
        P("gx", "gy"),
        P(),
        P(),
        P(),
        P(None, "gx", "gy"),
        P(("gx", "gy"), None),
        P(("gx", "gy"), None),
        P(("gx", "gy"), None),
        P(),
        P("gx", "gy", None),
        P("gx", "gy", None),
        P("gx", "gy", None),
        P(),
    )
    return jax.shard_map(
        local,
        mesh=mesh,
        in_specs=placed,
        out_specs=(P(None, None, "gx", "gy"), P(None, None, ("gx", "gy"), None), P("gx", "gy")),
        check_vma=False,
    )
```

```python
import jax
import jax.numpy as jnp
from jax import lax
from jax.experimental import pallas as pl
from jax.experimental.pallas import tpu as pltpu
from jax.sharding import PartitionSpec as P

V, NZ, BLK, CX, K, KI, NOPS, PB = 4, 8, 128, 256, 16, 4, 8, 16
VZ = V * NZ
F32, BF16 = jnp.float32, jnp.bfloat16
PAD = 8
CHUNK = 64
VMEM_BYTES = 32 * 1024 * 1024

X_ROWS, X_PAR, X_IDX, X_ALL = 0, 64, 128, 144
Y_COLS, Y_PAR, Y_RELAY, Y_IDX, Y_RIDX, Y_ALL = 0, 128, 192, 256, 272, 288

IN_HBM = pl.BlockSpec(memory_space=pltpu.HBM)
IN_VMEM = pl.BlockSpec(memory_space=pltpu.VMEM)
IN_SMEM = pl.BlockSpec(memory_space=pltpu.SMEM)
NT = (((1,), (1,)), ((), ()))
TN = (((0,), (0,)), ((), ()))


def exchange(value, axis, odd):
    pairs = []
    for a in range(odd, lax.axis_size(axis) - 1, 2):
        pairs += [(a, a + 1), (a + 1, a)]
    return lax.ppermute(value, axis, pairs)


def one_lower(value, axis):
    return lax.ppermute(value, axis, [(a, a - 1) for a in range(1, lax.axis_size(axis))])


def diagonal():
    nx, ny = lax.axis_size("gx"), lax.axis_size("gy")
    return [(i * ny + j, (i - 1) * ny + j - 1) for i in range(1, nx) for j in range(1, ny)]


def split(value):
    high = value.astype(BF16)
    return high, (value - high.astype(F32)).astype(BF16)


def lanes(shape):
    return lax.broadcasted_iota(jnp.int32, shape, len(shape) - 1)


def rows_kernel(parity, child, parent, tile, row, op, even, odd, first, last, blocks, names, stage, sems):
    copies = [
        pltpu.make_async_copy(child.at[:, pl.ds(0, 8)], first, sems.at[0]),
        pltpu.make_async_copy(child.at[:, pl.ds(CX - 8, 8)], last, sems.at[1]),
        pltpu.make_async_copy(parent, blocks, sems.at[2]),
    ] + [pltpu.make_async_copy(a, names.at[i], sems.at[3 + i]) for i, a in enumerate((tile, row, op))]
    for c in copies:
        c.start()
    stage[...] = jnp.zeros_like(stage)
    for c in copies:
        c.wait()
    for i in range(3):
        stage[i, :, 0:K] = names[i].astype(F32)
    index = stage[0] + pltpu.roll(stage[1], K, 1) + pltpu.roll(stage[2], 2 * K, 1)
    flag = parity[0] == 0
    for buffer in (even, odd):
        buffer[X_PAR:X_IDX] = blocks[...]
        buffer[X_IDX:X_ALL] = index
    for vz in range(VZ):
        low, high = first[vz, 0:2], last[vz, 6:8]
        even[2 * vz : 2 * vz + 2] = jnp.where(flag, high, low)
        odd[2 * vz : 2 * vz + 2] = jnp.where(flag, low, high)


def edges_kernel(child, fine_bank, coarse_bank, code, cells, to_next, to_prev, banks, coarse_banks, counts, fine, coarse, sems):
    copies = [
        pltpu.make_async_copy(child.at[pl.ds(NZ * v, NZ)], cells.at[pl.ds(NZ * v, NZ), pl.ds(PAD, CX)], sems.at[v])
        for v in range(V)
    ] + [pltpu.make_async_copy(fine_bank, fine, sems.at[V]), pltpu.make_async_copy(coarse_bank, coarse, sems.at[V + 1])]
    for c in copies:
        c.start()
    for vz in range(VZ):
        cells[vz, 0:PAD] = jnp.zeros((PAD, BLK), F32)
        cells[vz, PAD + CX : PAD + CX + PAD] = jnp.zeros((PAD, BLK), F32)
    wanted = lax.broadcasted_iota(jnp.int32, (512, CX), 0)
    total = jnp.zeros((512, CX), F32)
    for k in range(KI):
        total = total + jnp.where(code[k : k + 1, :] == wanted, 1.0, 0.0)
    counts[...] = total.T.astype(BF16)
    which = lanes((CX, BLK)) // 4
    edges = jnp.zeros((CX, BLK), F32)
    for v in range(V):
        copies[v].wait()
        for z in range(NZ):
            vz = NZ * v + z
            edges = jnp.where(which == vz, pltpu.roll(cells[vz, PAD : PAD + CX], (4 * vz + 2) % BLK, 1), edges)
    half = CX // 2
    upper = lanes((half, BLK)) % 4 >= 2
    to_next[...] = jnp.where(upper, pltpu.roll(edges[half:], 2, 1), edges[:half])
    to_prev[...] = jnp.where(upper, edges[:half], pltpu.roll(edges[half:], BLK - 2, 1))
    copies[V].wait()
    copies[V + 1].wait()
    for o in range(NOPS):
        high, low = split(fine[o])
        banks[0:BLK, BLK * o : BLK * (o + 1)] = high
        banks[BLK : 2 * BLK, BLK * o : BLK * (o + 1)] = low
        high, low = split(coarse[o])
        coarse_banks[0, BLK * o : BLK * (o + 1)] = high
        coarse_banks[1, BLK * o : BLK * (o + 1)] = low


def join_kernel(parity, even_x, odd_x, own_even, to_next, to_prev, even, odd):
    flag_x, flag = parity[0] == 0, parity[1] == 0
    even[Y_COLS:Y_PAR] = jnp.where(flag, to_next[...], to_prev[...])
    odd[Y_COLS:Y_PAR] = jnp.where(flag, to_prev[...], to_next[...])
    relay = jnp.where(flag_x, odd_x[X_PAR:X_ALL], even_x[X_PAR:X_ALL])
    own = own_even[X_PAR:X_ALL]
    for buffer in (even, odd):
        buffer[Y_PAR:Y_RELAY] = own[:64]
        buffer[Y_RELAY:Y_IDX] = relay[:64]
        buffer[Y_IDX:Y_RIDX] = own[64:]
        buffer[Y_RIDX:Y_ALL] = relay[64:]


def coefficients(courant):
    size = jnp.abs(courant)
    half = 0.5 * size
    return half * size - 1.5 * size, 2.0 * size - size * size, half * size - half


def inner_kernel(courant_x, courant_y, diffusion, cells, after, inner):
    del after
    lane = lanes((8, BLK))[0:1]

    def variable(v, carry):
        d = diffusion[v]
        for z in range(NZ):
            sx, sy = courant_x[z], courant_y[z]
            own_x, near_x, far_x = coefficients(sx)
            own_y, near_y, far_y = coefficients(sy)
            up_x, up_y = sx >= 0.0, sy >= 0.0
            own = 1.0 + own_x + own_y - 6.0 * d
            low_x = d + jnp.where(up_x, near_x, 0.0)
            high_x = d + jnp.where(up_x, 0.0, near_x)
            low_far = jnp.where(up_x, far_x, 0.0)
            high_far = jnp.where(up_x, 0.0, far_x)
            low_y = jnp.where(lane == 0, 0.0, d + jnp.where(up_y, near_y, 0.0))
            high_y = jnp.where(lane == BLK - 1, 0.0, d + jnp.where(up_y, 0.0, near_y))
            outside = jnp.where(up_y, 0, BLK - 2)
            far = jnp.where((lane >= outside) & (lane < outside + 2), 0.0, far_y)
            turn_far = jnp.where(up_y, 2, BLK - 2)
            vz = NZ * v + z
            for r in range(PAD, PAD + CX, CHUNK):
                c = cells[vz, r : r + CHUNK]
                total = own * c
                total = total + low_x * cells[vz, r - 1 : r - 1 + CHUNK]
                total = total + high_x * cells[vz, r + 1 : r + 1 + CHUNK]
                total = total + low_far * cells[vz, r - 2 : r - 2 + CHUNK]
                total = total + high_far * cells[vz, r + 2 : r + 2 + CHUNK]
                total = total + low_y * pltpu.roll(c, 1, 1)
                total = total + high_y * pltpu.roll(c, BLK - 1, 1)
                total = total + far * pltpu.roll(c, turn_far, 1)
                beside = None
                if z < NZ - 1:
                    beside = cells[vz + 1, r : r + CHUNK]
                if z > 0:
                    below = cells[vz - 1, r : r + CHUNK]
                    beside = below if beside is None else beside + below
                inner[vz, r - PAD : r - PAD + CHUNK] = total + d * beside
        return carry

    lax.fori_loop(0, V, variable, 0)


def per_level(values, level):
    out = jnp.zeros(level.shape, F32)
    for z in range(NZ):
        out = jnp.where(level == z, values[z], out)
    return out


def main_kernel(
    parity, courant_x, courant_y, diffusion,
    inner, building, own_x, even_x, odd_x, even_y, odd_y, banks, coarse_banks, counts,
    states, ground, part_own, part_x, part_y, part_both,
    new, walls, above_fix, below_fix, side_fix, select, ghost, table, fields, picked_high, picked_low, wall_sem, out_sems,
):
    flag_x, flag_y = parity[0] == 0, parity[1] == 0
    walls_in = pltpu.make_async_copy(building, walls, wall_sem)
    walls_in.start()

    prev_x = jnp.where(flag_x, odd_x[...], even_x[...])
    prev_y = jnp.where(flag_y, odd_y[...], even_y[...])
    parents = [own_x[X_PAR:X_IDX], prev_x[X_PAR:X_IDX], prev_y[Y_PAR:Y_RELAY], prev_y[Y_RELAY:Y_IDX]]
    indices = [own_x[X_IDX:X_ALL], prev_x[X_IDX:X_ALL], prev_y[Y_IDX:Y_RIDX], prev_y[Y_RIDX:Y_ALL]]

    def weights(courant, level, variable):
        d = jnp.zeros(level.shape, F32)
        for v in range(V):
            d = jnp.where(variable == v, diffusion[v], d)
        s = per_level(courant, level)
        _, near, far = coefficients(s)
        up = s >= 0.0
        return (
            d + jnp.where(up, near, 0.0), d + jnp.where(up, 0.0, near), jnp.where(up, far, 0.0), jnp.where(up, 0.0, far),
        )

    next_rows = jnp.where(flag_x, even_x[X_ROWS:X_PAR], odd_x[X_ROWS:X_PAR])
    prev_rows = prev_x[X_ROWS:X_PAR]
    line = lax.broadcasted_iota(jnp.int32, (2 * VZ, BLK), 0)
    low, high, low_far, high_far = weights(courant_x, (line // 2) % NZ, line // (2 * NZ))
    first = line % 2 == 0
    above_fix[...] = low_far * prev_rows + jnp.where(first, low * pltpu.roll(prev_rows, 2 * VZ - 1, 0), 0.0)
    below_fix[...] = high_far * next_rows + jnp.where(first, 0.0, high * pltpu.roll(next_rows, 1, 0))

    half = CX // 2
    next_y = jnp.where(flag_y, even_y[Y_COLS:Y_PAR], odd_y[Y_COLS:Y_PAR])
    before = prev_y[Y_COLS:Y_PAR]
    upper = lanes((half, BLK)) % 4 >= 2
    lane = lanes((8, BLK))
    low, high, low_far, high_far = (w[0:1] for w in weights(courant_y, (lane // 4) % NZ, lane // (4 * NZ)))
    place = lane[0:1] % 4
    by_minus_2 = jnp.where(place < 2, high_far, 0.0)
    by_minus_1 = jnp.where(place == 1, high, 0.0)
    by_plus_1 = jnp.where(place == 2, low, 0.0)
    by_plus_2 = jnp.where(place >= 2, low_far, 0.0)
    for part in range(2):
        if part == 0:
            columns = jnp.where(upper, next_y, before)
        else:
            columns = jnp.where(upper, pltpu.roll(next_y, 2, 1), pltpu.roll(before, BLK - 2, 1))
        side_fix[half * part : half * (part + 1)] = (
            by_minus_2 * pltpu.roll(columns, BLK - 2, 1)
            + by_minus_1 * pltpu.roll(columns, BLK - 1, 1)
            + by_plus_1 * pltpu.roll(columns, 1, 1)
            + by_plus_2 * pltpu.roll(columns, 2, 1)
        )

    high, low = split(jnp.concatenate([parents[t][PB * v : PB * (v + 1)] for v in range(V) for t in range(4)], axis=0))
    for o in range(NOPS):
        bank_high, bank_low = (coarse_banks[i, BLK * o : BLK * (o + 1)] for i in range(2))
        made = (
            lax.dot_general(high, bank_high, NT, preferred_element_type=F32)
            + lax.dot_general(high, bank_low, NT, preferred_element_type=F32)
            + lax.dot_general(low, bank_high, NT, preferred_element_type=F32)
        )
        made_high, made_low = split(made)
        for v in range(V):
            table[64 * o : 64 * (o + 1), BLK * v : BLK * (v + 1)] = made_high[64 * v : 64 * (v + 1)]
            table[512 + 64 * o : 512 + 64 * (o + 1), BLK * v : BLK * (v + 1)] = made_low[64 * v : 64 * (v + 1)]
    ghost[...] = jnp.dot(counts[...], table[0:512], preferred_element_type=F32) + jnp.dot(
        counts[...], table[512:1024], preferred_element_type=F32
    )

    codes = []
    for t in range(4):
        names = indices[t]
        rows = pltpu.roll(names, BLK - K, 1)
        ops = pltpu.roll(names, BLK - 2 * K, 1)
        codes.append(jnp.where(names == float(t), ops * float(CX) + rows, -1.0))
    codes = jnp.concatenate(codes, axis=0)
    spread = [jnp.broadcast_to(codes[:, k : k + 1], (64, CX)) for k in range(K)]
    cell = lanes((64, CX)).astype(F32)
    for o in range(NOPS):
        total = jnp.zeros((64, CX), F32)
        for k in range(K):
            total = total + jnp.where(spread[k] == cell + float(CX * o), 1.0, 0.0)
        total = total.astype(BF16)
        select[64 * o : 64 * (o + 1), 0:CX] = total
        select[64 * o : 64 * (o + 1), CX : 2 * CX] = total

    walls_in.wait()
    at_edge = (lanes((CHUNK, BLK)) + 2) % BLK < 4
    no_rows = jnp.zeros((6, BLK), F32)

    def variable(v, carry):
        d = diffusion[v]
        for z in range(NZ):
            vz = NZ * v + z
            turn = (2 * BLK - 2 - 4 * vz) % BLK
            for r in range(0, CX, CHUNK):
                total = inner[vz, r : r + CHUNK]
                total = total + jnp.where(at_edge, pltpu.roll(side_fix[r : r + CHUNK], turn, 1), 0.0)
                if z == NZ - 1:
                    total = total + d * ghost[r : r + CHUNK, pl.ds(pl.multiple_of(BLK * v, BLK), BLK)]
                if r == 0:
                    fix = jnp.concatenate([above_fix[pl.ds(2 * vz, 2)], no_rows], axis=0)
                    total = jnp.concatenate([total[:8] + fix, total[8:]], axis=0)
                if r == CX - CHUNK:
                    fix = jnp.concatenate([no_rows, below_fix[pl.ds(2 * vz, 2)]], axis=0)
                    total = jnp.concatenate([total[:-8], total[-8:] + fix], axis=0)
                total = jnp.where(walls[z, r : r + CHUNK] == 1, 0.0, total)
                new[vz, r : r + CHUNK] = total
                high, low = split(total)
                fields[r : r + CHUNK, BLK * z : BLK * (z + 1)] = high
                fields[CX + r : CX + r + CHUNK, BLK * z : BLK * (z + 1)] = low
                if z == 0:
                    ground[v, r : r + CHUNK] = total
        pltpu.make_async_copy(new.at[pl.ds(NZ * v, NZ)], states.at[pl.ds(NZ * v, NZ)], out_sems.at[v]).start()
        for z in range(0, NZ, 2):
            found = jnp.dot(select[...], fields[:, BLK * z : BLK * (z + 2)], preferred_element_type=F32)
            high, low = split(found)
            for o in range(NOPS):
                for e in range(2):
                    to = (slice(64 * (z + e), 64 * (z + e + 1)), slice(BLK * o, BLK * (o + 1)))
                    at = (slice(64 * o, 64 * (o + 1)), slice(BLK * e, BLK * (e + 1)))
                    picked_high[to] = high[at]
                    picked_low[to] = low[at]
        both = lax.dot_general(picked_high[...], banks[...], NT, preferred_element_type=F32)
        rest = lax.dot_general(picked_low[...], banks[0:BLK], NT, preferred_element_type=F32)
        result = both[:, :BLK] + both[:, BLK:] + rest
        for z in range(NZ):
            at = pl.ds(pl.multiple_of(PB * (NZ * v + z), PB), PB)
            for i, part in enumerate((part_own, part_x, part_y, part_both)):
                part[at] = result[64 * z + PB * i : 64 * z + PB * (i + 1)]
        return carry

    lax.fori_loop(0, V, variable, 0)
    for v in range(V):
        pltpu.make_async_copy(new.at[pl.ds(NZ * v, NZ)], states.at[pl.ds(NZ * v, NZ)], out_sems.at[v]).wait()


def comfort_kernel(ground, radiant, slab, part_own, comfort, so_far):
    u, w, t, h = (ground[v] for v in range(V))
    speed = jnp.sqrt(u * u + w * w + 0.25)
    excess = radiant[...] - t
    comfort[...] = t + 0.3 * excess - 0.6 * (speed - 1.0) + 0.4 * h + 0.1 * t * excess - 0.15 * speed * excess
    so_far[...] = 0.5 * slab[...] + 0.5 * part_own[...]


def shape(*dims, kind=F32):
    return jax.ShapeDtypeStruct(dims, kind)


def local(
    child_state, parent_slab, parent_above, radiative_mean_kelvin, courant_x, courant_y, diffusion, building,
    fine_tile, fine_row, fine_op, fine_bank, coarse_tile, coarse_row, coarse_op, coarse_bank,
):
    parity = jnp.stack([lax.axis_index("gx") % 2, lax.axis_index("gy") % 2]).astype(jnp.int32)
    child = child_state.reshape(VZ, CX, BLK)
    parent = parent_above.reshape(V * PB, BLK)
    params = pltpu.CompilerParams(vmem_limit_bytes=VMEM_BYTES)
    x_even, x_odd = pl.pallas_call(
        rows_kernel,
        out_shape=(shape(X_ALL, BLK), shape(X_ALL, BLK)),
        in_specs=[IN_SMEM] + [IN_HBM] * 5,
        out_specs=(IN_VMEM,) * 2,
        scratch_shapes=[
            pltpu.VMEM((VZ, 8, BLK), F32), pltpu.VMEM((VZ, 8, BLK), F32), pltpu.VMEM((V * PB, BLK), F32),
            pltpu.VMEM((3, PB, K), jnp.int32), pltpu.VMEM((3, PB, BLK), F32), pltpu.SemaphoreType.DMA((6,)),
        ],
        compiler_params=pltpu.CompilerParams(vmem_limit_bytes=56 * 1024 * 1024),
    )(parity, child, parent, fine_tile, fine_row, fine_op)
    got_x_even = exchange(x_even, "gx", 0)
    got_x_odd = exchange(x_odd, "gx", 1)
    coarse_code = (coarse_op * 64 + coarse_tile * PB + coarse_row).reshape(CX, KI).T
    cells, to_next, to_prev, banks, coarse_banks, counts = pl.pallas_call(
        edges_kernel,
        out_shape=(
            shape(VZ, CX + 2 * PAD, BLK), shape(CX // 2, BLK), shape(CX // 2, BLK),
            shape(2 * BLK, NOPS * BLK, kind=BF16), shape(2, NOPS * BLK, BLK, kind=BF16), shape(CX, 512, kind=BF16),
        ),
        in_specs=[IN_HBM] * 3 + [IN_VMEM],
        out_specs=(IN_VMEM,) * 6,
        scratch_shapes=[
            pltpu.VMEM((NOPS, BLK, BLK), F32), pltpu.VMEM((NOPS, BLK, BLK), F32), pltpu.SemaphoreType.DMA((V + 2,)),
        ],
        compiler_params=params,
    )(child, fine_bank, coarse_bank, coarse_code)
    y_even, y_odd = pl.pallas_call(
        join_kernel,
        out_shape=(shape(Y_ALL, BLK), shape(Y_ALL, BLK)),
        in_specs=[IN_SMEM] + [IN_VMEM] * 5,
        out_specs=(IN_VMEM,) * 2,
        compiler_params=params,
    )(parity, got_x_even, got_x_odd, x_even, to_next, to_prev)
    got_y_odd = exchange(y_odd, "gy", 1)
    got_y_even = exchange(y_even, "gy", 0)
    inner = pl.pallas_call(
        inner_kernel,
        out_shape=shape(VZ, CX, BLK),
        in_specs=[IN_SMEM] * 3 + [IN_VMEM, pl.BlockSpec(memory_space=pl.ANY)],
        out_specs=IN_VMEM,
        compiler_params=params,
    )(courant_x, courant_y, diffusion, cells, y_even)
    states, ground, part_own, part_x, part_y, part_both = pl.pallas_call(
        main_kernel,
        out_shape=(shape(VZ, CX, BLK), shape(V, CX, BLK)) + (shape(VZ * PB, BLK),) * 4,
        in_specs=[IN_SMEM] * 4 + [IN_VMEM, IN_HBM] + [IN_VMEM] * 8,
        out_specs=(IN_HBM,) + (IN_VMEM,) * 5,
        scratch_shapes=[
            pltpu.VMEM((VZ, CX, BLK), F32),
            pltpu.VMEM((NZ, CX, BLK), jnp.int32),
            pltpu.VMEM((2 * VZ, BLK), F32),
            pltpu.VMEM((2 * VZ, BLK), F32),
            pltpu.VMEM((CX, BLK), F32),
            pltpu.VMEM((512, 2 * CX), BF16),
            pltpu.VMEM((CX, V * BLK), F32),
            pltpu.VMEM((1024, V * BLK), BF16),
            pltpu.VMEM((2 * CX, NZ * BLK), BF16),
            pltpu.VMEM((512, NOPS * BLK), BF16),
            pltpu.VMEM((512, NOPS * BLK), BF16),
            pltpu.SemaphoreType.DMA,
            pltpu.SemaphoreType.DMA((V,)),
        ],
        compiler_params=params,
    )(
        parity, courant_x, courant_y, diffusion,
        inner, building, x_even, got_x_even, got_x_odd, got_y_even, got_y_odd, banks, coarse_banks, counts,
    )
    got_both = lax.ppermute(part_both, ("gx", "gy"), diagonal())
    got_x = one_lower(part_x, "gx")
    got_y = one_lower(part_y, "gy")
    comfort, so_far = pl.pallas_call(
        comfort_kernel,
        out_shape=(shape(CX, BLK), shape(VZ * PB, BLK)),
        in_specs=[IN_VMEM] * 4,
        out_specs=(IN_VMEM,) * 2,
        compiler_params=params,
    )(ground, radiative_mean_kelvin, parent_slab.reshape(VZ * PB, BLK), part_own)
    parent_new = so_far + 0.5 * (got_y + got_x + got_both)
    return states.reshape(child_state.shape), parent_new.reshape(parent_slab.shape), comfort


def solution(mesh):
    placed = (
        P(None, None, "gx", "gy"),
        P(None, None, ("gx", "gy"), None),
        P(None, ("gx", "gy"), None),
        P("gx", "gy"),
        P(),
        P(),
        P(),
        P(None, "gx", "gy"),
        P(("gx", "gy"), None),
        P(("gx", "gy"), None),
        P(("gx", "gy"), None),
        P(),
        P("gx", "gy", None),
        P("gx", "gy", None),
        P("gx", "gy", None),
        P(),
    )
    return jax.shard_map(
        local,
        mesh=mesh,
        in_specs=placed,
        out_specs=(P(None, None, "gx", "gy"), P(None, None, ("gx", "gy"), None), P("gx", "gy")),
        check_vma=False,
    )
```

```python
import jax
import jax.numpy as jnp
from jax import lax
from jax.experimental import pallas as pl
from jax.experimental.pallas import tpu as pltpu
from jax.sharding import PartitionSpec as P

V, NZ, BLK, CX, K, KI, NOPS, PB = 4, 8, 128, 256, 16, 4, 8, 16
VZ = V * NZ
F32, BF16 = jnp.float32, jnp.bfloat16
PAD = 8
CHUNK = 64
VMEM_BYTES = 32 * 1024 * 1024

X_ROWS, X_PAR, X_IDX, X_ALL = 0, 64, 128, 144
Y_COLS, Y_PAR, Y_RELAY, Y_IDX, Y_RIDX, Y_ALL = 0, 128, 192, 256, 272, 288

IN_HBM = pl.BlockSpec(memory_space=pltpu.HBM)
IN_VMEM = pl.BlockSpec(memory_space=pltpu.VMEM)
IN_SMEM = pl.BlockSpec(memory_space=pltpu.SMEM)
NT = (((1,), (1,)), ((), ()))
TN = (((0,), (0,)), ((), ()))


def exchange(value, axis, odd):
    pairs = []
    for a in range(odd, lax.axis_size(axis) - 1, 2):
        pairs += [(a, a + 1), (a + 1, a)]
    return lax.ppermute(value, axis, pairs)


def one_lower(value, axis):
    return lax.ppermute(value, axis, [(a, a - 1) for a in range(1, lax.axis_size(axis))])


def split(value):
    high = value.astype(BF16)
    return high, (value - high.astype(F32)).astype(BF16)


def lanes(shape):
    return lax.broadcasted_iota(jnp.int32, shape, len(shape) - 1)


def rows_kernel(child, parent, tile, row, op, even, odd, first, last, blocks, names, stage, sems):
    copies = [
        pltpu.make_async_copy(child.at[:, pl.ds(0, 8)], first, sems.at[0]),
        pltpu.make_async_copy(child.at[:, pl.ds(CX - 8, 8)], last, sems.at[1]),
        pltpu.make_async_copy(parent, blocks, sems.at[2]),
    ] + [pltpu.make_async_copy(a, names.at[i], sems.at[3 + i]) for i, a in enumerate((tile, row, op))]
    for c in copies:
        c.start()
    stage[...] = jnp.zeros_like(stage)
    for c in copies:
        c.wait()
    for i in range(3):
        stage[i, :, 0:K] = names[i].astype(F32)
    index = stage[0] + pltpu.roll(stage[1], K, 1) + pltpu.roll(stage[2], 2 * K, 1)
    flag = lax.axis_index("gx") % 2 == 0
    for buffer in (even, odd):
        buffer[X_PAR:X_IDX] = blocks[...]
        buffer[X_IDX:X_ALL] = index
    for vz in range(VZ):
        low, high = first[vz, 0:2], last[vz, 6:8]
        even[2 * vz : 2 * vz + 2] = jnp.where(flag, high, low)
        odd[2 * vz : 2 * vz + 2] = jnp.where(flag, low, high)


def edges_kernel(child, fine_bank, coarse_bank, code, cells, to_next, to_prev, banks, coarse_banks, counts, fine, coarse, sems):
    copies = [
        pltpu.make_async_copy(child.at[pl.ds(NZ * v, NZ)], cells.at[pl.ds(NZ * v, NZ), pl.ds(PAD, CX)], sems.at[v])
        for v in range(V)
    ] + [pltpu.make_async_copy(fine_bank, fine, sems.at[V]), pltpu.make_async_copy(coarse_bank, coarse, sems.at[V + 1])]
    for c in copies:
        c.start()
    for vz in range(VZ):
        cells[vz, 0:PAD] = jnp.zeros((PAD, BLK), F32)
        cells[vz, PAD + CX : PAD + CX + PAD] = jnp.zeros((PAD, BLK), F32)
    wanted = lax.broadcasted_iota(jnp.int32, (512, CX), 0)
    total = jnp.zeros((512, CX), F32)
    for k in range(KI):
        total = total + jnp.where(code[k : k + 1, :] == wanted, 1.0, 0.0)
    counts[...] = total.T.astype(BF16)
    which = lanes((CX, BLK)) // 4
    edges = jnp.zeros((CX, BLK), F32)
    for v in range(V):
        copies[v].wait()
        for z in range(NZ):
            vz = NZ * v + z
            edges = jnp.where(which == vz, pltpu.roll(cells[vz, PAD : PAD + CX], (4 * vz + 2) % BLK, 1), edges)
    half = CX // 2
    upper = lanes((half, BLK)) % 4 >= 2
    to_next[...] = jnp.where(upper, pltpu.roll(edges[half:], 2, 1), edges[:half])
    to_prev[...] = jnp.where(upper, edges[:half], pltpu.roll(edges[half:], BLK - 2, 1))
    copies[V].wait()
    copies[V + 1].wait()
    for o in range(NOPS):
        high, low = split(fine[o])
        banks[0:BLK, BLK * o : BLK * (o + 1)] = high
        banks[BLK : 2 * BLK, BLK * o : BLK * (o + 1)] = low
        high, low = split(coarse[o])
        coarse_banks[0, BLK * o : BLK * (o + 1)] = high
        coarse_banks[1, BLK * o : BLK * (o + 1)] = low


def join_kernel(even_x, odd_x, own_even, to_next, to_prev, even, odd):
    flag_x, flag = lax.axis_index("gx") % 2 == 0, lax.axis_index("gy") % 2 == 0
    even[Y_COLS:Y_PAR] = jnp.where(flag, to_next[...], to_prev[...])
    odd[Y_COLS:Y_PAR] = jnp.where(flag, to_prev[...], to_next[...])
    relay = jnp.where(flag_x, odd_x[X_PAR:X_ALL], even_x[X_PAR:X_ALL])
    own = own_even[X_PAR:X_ALL]
    for buffer in (even, odd):
        buffer[Y_PAR:Y_RELAY] = own[:64]
        buffer[Y_RELAY:Y_IDX] = relay[:64]
        buffer[Y_IDX:Y_RIDX] = own[64:]
        buffer[Y_RIDX:Y_ALL] = relay[64:]


def coefficients(courant):
    size = jnp.abs(courant)
    half = 0.5 * size
    return half * size - 1.5 * size, 2.0 * size - size * size, half * size - half


def inner_kernel(courant_x, courant_y, diffusion, cells, after, inner):
    del after
    lane = lanes((8, BLK))[0:1]

    def variable(v, carry):
        d = diffusion[v]
        for z in range(NZ):
            sx, sy = courant_x[z], courant_y[z]
            own_x, near_x, far_x = coefficients(sx)
            own_y, near_y, far_y = coefficients(sy)
            up_x, up_y = sx >= 0.0, sy >= 0.0
            own = 1.0 + own_x + own_y - 6.0 * d
            low_x = d + jnp.where(up_x, near_x, 0.0)
            high_x = d + jnp.where(up_x, 0.0, near_x)
            low_far = jnp.where(up_x, far_x, 0.0)
            high_far = jnp.where(up_x, 0.0, far_x)
            low_y = jnp.where(lane == 0, 0.0, d + jnp.where(up_y, near_y, 0.0))
            high_y = jnp.where(lane == BLK - 1, 0.0, d + jnp.where(up_y, 0.0, near_y))
            outside = jnp.where(up_y, 0, BLK - 2)
            far = jnp.where((lane >= outside) & (lane < outside + 2), 0.0, far_y)
            turn_far = jnp.where(up_y, 2, BLK - 2)
            vz = NZ * v + z
            for r in range(PAD, PAD + CX, CHUNK):
                c = cells[vz, r : r + CHUNK]
                total = own * c
                total = total + low_x * cells[vz, r - 1 : r - 1 + CHUNK]
                total = total + high_x * cells[vz, r + 1 : r + 1 + CHUNK]
                total = total + low_far * cells[vz, r - 2 : r - 2 + CHUNK]
                total = total + high_far * cells[vz, r + 2 : r + 2 + CHUNK]
                total = total + low_y * pltpu.roll(c, 1, 1)
                total = total + high_y * pltpu.roll(c, BLK - 1, 1)
                total = total + far * pltpu.roll(c, turn_far, 1)
                beside = None
                if z < NZ - 1:
                    beside = cells[vz + 1, r : r + CHUNK]
                if z > 0:
                    below = cells[vz - 1, r : r + CHUNK]
                    beside = below if beside is None else beside + below
                inner[vz, r - PAD : r - PAD + CHUNK] = total + d * beside
        return carry

    lax.fori_loop(0, V, variable, 0)


def per_level(values, level):
    out = jnp.zeros(level.shape, F32)
    for z in range(NZ):
        out = jnp.where(level == z, values[z], out)
    return out


def choose(names, tile, select, at=0):
    rows = pltpu.roll(names, BLK - K, 1)
    ops = pltpu.roll(names, BLK - 2 * K, 1)
    codes = jnp.where(names == float(tile), ops * float(CX) + rows, -1.0)
    spread = [jnp.broadcast_to(codes[:, k : k + 1], (PB, CX)) for k in range(K)]
    cell = lanes((PB, CX)).astype(F32)
    for o in range(NOPS):
        total = jnp.zeros((PB, CX), F32)
        for k in range(K):
            total = total + jnp.where(spread[k] == cell + float(CX * o), 1.0, 0.0)
        total = total.astype(BF16)
        row = (select.shape[0] // NOPS) * o + PB * at
        select[row : row + PB, 0:CX] = total
        select[row : row + PB, CX : 2 * CX] = total


def gather(select, pair, vz, picked):
    many = select.shape[0] // NOPS
    found = jnp.dot(select[...], pair, preferred_element_type=F32)
    for part, value in enumerate(split(found)):
        for o in range(NOPS):
            for e in range(2):
                picked[part, pl.ds(pl.multiple_of(many * (vz + e), many), many), BLK * o : BLK * (o + 1)] = value[
                    many * o : many * (o + 1), BLK * e : BLK * (e + 1)
                ]


def through_banks(picked, banks):
    both = lax.dot_general(picked[0], banks[...], NT, preferred_element_type=F32)
    rest = lax.dot_general(picked[1], banks[0:BLK], NT, preferred_element_type=F32)
    return both[:, :BLK] + both[:, BLK:] + rest


def gather_all(select, fields, picked):
    def one_pair(i, carry):
        gather(select, fields[:, pl.ds(pl.multiple_of(2 * BLK * i, 2 * BLK), 2 * BLK)], 2 * i, picked)
        return carry

    lax.fori_loop(0, VZ // 2, one_pair, 0, unroll=4)


def update_kernel(
    courant_x, courant_y, diffusion,
    inner, walls, own_x, even_x, odd_x, even_y, odd_y, banks, coarse_banks, counts,
    new, fields, part_both,
    above_fix, below_fix, side_fix, select, ghost, table, picked,
):
    flag_x, flag_y = lax.axis_index("gx") % 2 == 0, lax.axis_index("gy") % 2 == 0

    prev_x = jnp.where(flag_x, odd_x[...], even_x[...])
    prev_y = jnp.where(flag_y, odd_y[...], even_y[...])
    parents = [own_x[X_PAR:X_IDX], prev_x[X_PAR:X_IDX], prev_y[Y_PAR:Y_RELAY], prev_y[Y_RELAY:Y_IDX]]

    def weights(courant, level, variable):
        d = jnp.zeros(level.shape, F32)
        for v in range(V):
            d = jnp.where(variable == v, diffusion[v], d)
        s = per_level(courant, level)
        _, near, far = coefficients(s)
        up = s >= 0.0
        return (
            d + jnp.where(up, near, 0.0), d + jnp.where(up, 0.0, near), jnp.where(up, far, 0.0), jnp.where(up, 0.0, far),
        )

    next_rows = jnp.where(flag_x, even_x[X_ROWS:X_PAR], odd_x[X_ROWS:X_PAR])
    prev_rows = prev_x[X_ROWS:X_PAR]
    line = lax.broadcasted_iota(jnp.int32, (2 * VZ, BLK), 0)
    low, high, low_far, high_far = weights(courant_x, (line // 2) % NZ, line // (2 * NZ))
    first = line % 2 == 0
    above_fix[...] = low_far * prev_rows + jnp.where(first, low * pltpu.roll(prev_rows, 2 * VZ - 1, 0), 0.0)
    below_fix[...] = high_far * next_rows + jnp.where(first, 0.0, high * pltpu.roll(next_rows, 1, 0))

    half = CX // 2
    next_y = jnp.where(flag_y, even_y[Y_COLS:Y_PAR], odd_y[Y_COLS:Y_PAR])
    before = prev_y[Y_COLS:Y_PAR]
    upper = lanes((half, BLK)) % 4 >= 2
    lane = lanes((8, BLK))
    low, high, low_far, high_far = (w[0:1] for w in weights(courant_y, (lane // 4) % NZ, lane // (4 * NZ)))
    place = lane[0:1] % 4
    by_minus_2 = jnp.where(place < 2, high_far, 0.0)
    by_minus_1 = jnp.where(place == 1, high, 0.0)
    by_plus_1 = jnp.where(place == 2, low, 0.0)
    by_plus_2 = jnp.where(place >= 2, low_far, 0.0)
    for part in range(2):
        if part == 0:
            columns = jnp.where(upper, next_y, before)
        else:
            columns = jnp.where(upper, pltpu.roll(next_y, 2, 1), pltpu.roll(before, BLK - 2, 1))
        side_fix[half * part : half * (part + 1)] = (
            by_minus_2 * pltpu.roll(columns, BLK - 2, 1)
            + by_minus_1 * pltpu.roll(columns, BLK - 1, 1)
            + by_plus_1 * pltpu.roll(columns, 1, 1)
            + by_plus_2 * pltpu.roll(columns, 2, 1)
        )

    high, low = split(jnp.concatenate([parents[t][PB * v : PB * (v + 1)] for v in range(V) for t in range(4)], axis=0))
    for o in range(NOPS):
        bank_high, bank_low = (coarse_banks[i, BLK * o : BLK * (o + 1)] for i in range(2))
        made = (
            lax.dot_general(high, bank_high, NT, preferred_element_type=F32)
            + lax.dot_general(high, bank_low, NT, preferred_element_type=F32)
            + lax.dot_general(low, bank_high, NT, preferred_element_type=F32)
        )
        made_high, made_low = split(made)
        for v in range(V):
            table[64 * o : 64 * (o + 1), BLK * v : BLK * (v + 1)] = made_high[64 * v : 64 * (v + 1)]
            table[512 + 64 * o : 512 + 64 * (o + 1), BLK * v : BLK * (v + 1)] = made_low[64 * v : 64 * (v + 1)]
    ghost[...] = jnp.dot(counts[...], table[0:512], preferred_element_type=F32) + jnp.dot(
        counts[...], table[512:1024], preferred_element_type=F32
    )

    choose(prev_y[Y_RIDX:Y_ALL], 3, select)
    at_edge = (lanes((CHUNK, BLK)) + 2) % BLK < 4
    no_rows = jnp.zeros((6, BLK), F32)

    def variable(v, carry):
        d = diffusion[v]
        for z in range(NZ):
            vz = NZ * v + z
            turn = (2 * BLK - 2 - 4 * vz) % BLK
            for r in range(0, CX, CHUNK):
                total = inner[vz, r : r + CHUNK]
                total = total + jnp.where(at_edge, pltpu.roll(side_fix[r : r + CHUNK], turn, 1), 0.0)
                if z == NZ - 1:
                    total = total + d * ghost[r : r + CHUNK, pl.ds(pl.multiple_of(BLK * v, BLK), BLK)]
                if r == 0:
                    fix = jnp.concatenate([above_fix[pl.ds(2 * vz, 2)], no_rows], axis=0)
                    total = jnp.concatenate([total[:8] + fix, total[8:]], axis=0)
                if r == CX - CHUNK:
                    fix = jnp.concatenate([no_rows, below_fix[pl.ds(2 * vz, 2)]], axis=0)
                    total = jnp.concatenate([total[:-8], total[-8:] + fix], axis=0)
                total = jnp.where(walls[z, r : r + CHUNK] == 1, 0.0, total)
                new[vz, r : r + CHUNK] = total
                high, low = split(total)
                columns = pl.ds(pl.multiple_of(BLK * vz, BLK), BLK)
                fields[r : r + CHUNK, columns] = high
                fields[CX + r : CX + r + CHUNK, columns] = low
            if z % 2 == 1:
                pair = pl.ds(pl.multiple_of(BLK * (vz - 1), BLK), 2 * BLK)
                gather(select, fields[:, pair], vz - 1, picked)
        return carry

    lax.fori_loop(0, V, variable, 0)
    part_both[...] = through_banks(picked, banks)


def sides_kernel(even_x, odd_x, even_y, odd_y, fields, banks, part_x, part_y, select, picked):
    flag_x, flag_y = lax.axis_index("gx") % 2 == 0, lax.axis_index("gy") % 2 == 0
    choose(jnp.where(flag_x, odd_x[X_IDX:X_ALL], even_x[X_IDX:X_ALL]), 1, select, 0)
    choose(jnp.where(flag_y, odd_y[Y_IDX:Y_RIDX], even_y[Y_IDX:Y_RIDX]), 2, select, 1)
    gather_all(select, fields, picked)
    result = through_banks(picked, banks)
    for vz in range(VZ):
        part_x[PB * vz : PB * (vz + 1)] = result[2 * PB * vz : 2 * PB * vz + PB]
        part_y[PB * vz : PB * (vz + 1)] = result[2 * PB * vz + PB : 2 * PB * (vz + 1)]


def add_kernel(part_x, got_both, part_y, to_x, to_y):
    to_x[...] = part_x[...] + got_both[...]
    to_y[...] = part_y[...]


def own_kernel(own_x, new, fields, banks, radiant, slab, after, states, comfort, so_far, select, picked, sem):
    del after
    out = pltpu.make_async_copy(new, states, sem)
    out.start()
    choose(own_x[X_IDX:X_ALL], 0, select)
    gather_all(select, fields, picked)
    so_far[...] = 0.5 * slab[...] + 0.5 * through_banks(picked, banks)
    u, w, t, h = (new[NZ * v] for v in range(V))
    speed = jnp.sqrt(u * u + w * w + 0.25)
    excess = radiant[...] - t
    comfort[...] = t + 0.3 * excess - 0.6 * (speed - 1.0) + 0.4 * h + 0.1 * t * excess - 0.15 * speed * excess
    out.wait()


def shape(*dims, kind=F32):
    return jax.ShapeDtypeStruct(dims, kind)


def local(
    child_state, parent_slab, parent_above, radiative_mean_kelvin, courant_x, courant_y, diffusion, building,
    fine_tile, fine_row, fine_op, fine_bank, coarse_tile, coarse_row, coarse_op, coarse_bank,
):
    child = child_state.reshape(VZ, CX, BLK)
    parent = parent_above.reshape(V * PB, BLK)
    params = pltpu.CompilerParams(vmem_limit_bytes=VMEM_BYTES)
    x_even, x_odd = pl.pallas_call(
        rows_kernel,
        out_shape=(shape(X_ALL, BLK), shape(X_ALL, BLK)),
        in_specs=[IN_HBM] * 5,
        out_specs=(IN_VMEM,) * 2,
        scratch_shapes=[
            pltpu.VMEM((VZ, 8, BLK), F32), pltpu.VMEM((VZ, 8, BLK), F32), pltpu.VMEM((V * PB, BLK), F32),
            pltpu.VMEM((3, PB, K), jnp.int32), pltpu.VMEM((3, PB, BLK), F32), pltpu.SemaphoreType.DMA((6,)),
        ],
        compiler_params=pltpu.CompilerParams(vmem_limit_bytes=56 * 1024 * 1024),
    )(child, parent, fine_tile, fine_row, fine_op)
    got_x_even = exchange(x_even, "gx", 0)
    got_x_odd = exchange(x_odd, "gx", 1)
    coarse_code = (coarse_op * 64 + coarse_tile * PB + coarse_row).reshape(CX, KI).T
    cells, to_next, to_prev, banks, coarse_banks, counts = pl.pallas_call(
        edges_kernel,
        out_shape=(
            shape(VZ, CX + 2 * PAD, BLK), shape(CX // 2, BLK), shape(CX // 2, BLK),
            shape(2 * BLK, NOPS * BLK, kind=BF16), shape(2, NOPS * BLK, BLK, kind=BF16), shape(CX, 512, kind=BF16),
        ),
        in_specs=[IN_HBM] * 3 + [IN_VMEM],
        out_specs=(IN_VMEM,) * 6,
        scratch_shapes=[
            pltpu.VMEM((NOPS, BLK, BLK), F32), pltpu.VMEM((NOPS, BLK, BLK), F32), pltpu.SemaphoreType.DMA((V + 2,)),
        ],
        compiler_params=params,
    )(child, fine_bank, coarse_bank, coarse_code)
    y_even, y_odd = pl.pallas_call(
        join_kernel,
        out_shape=(shape(Y_ALL, BLK), shape(Y_ALL, BLK)),
        in_specs=[IN_VMEM] * 5,
        out_specs=(IN_VMEM,) * 2,
        compiler_params=params,
    )(got_x_even, got_x_odd, x_even, to_next, to_prev)
    got_y_odd = exchange(y_odd, "gy", 1)
    got_y_even = exchange(y_even, "gy", 0)
    inner = pl.pallas_call(
        inner_kernel,
        out_shape=shape(VZ, CX, BLK),
        in_specs=[IN_SMEM] * 3 + [IN_VMEM, pl.BlockSpec(memory_space=pl.ANY)],
        out_specs=IN_VMEM,
        compiler_params=params,
    )(courant_x, courant_y, diffusion, cells, y_even)
    fields_shape = shape(2 * CX, VZ * BLK, kind=BF16)
    select_and_picked = [pltpu.VMEM((NOPS * PB, 2 * CX), BF16), pltpu.VMEM((2, VZ * PB, NOPS * BLK), BF16)]
    new, fields, part_both = pl.pallas_call(
        update_kernel,
        out_shape=(shape(VZ, CX, BLK), fields_shape, shape(VZ * PB, BLK)),
        in_specs=[IN_SMEM] * 3 + [IN_VMEM] * 2 + [IN_VMEM] * 8,
        out_specs=(IN_VMEM,) * 3,
        input_output_aliases={3: 0},
        scratch_shapes=[
            pltpu.VMEM((2 * VZ, BLK), F32),
            pltpu.VMEM((2 * VZ, BLK), F32),
            pltpu.VMEM((CX, BLK), F32),
            select_and_picked[0],
            pltpu.VMEM((CX, V * BLK), F32),
            pltpu.VMEM((1024, V * BLK), BF16),
            select_and_picked[1],
        ],
        compiler_params=params,
    )(
        courant_x, courant_y, diffusion,
        inner, building, x_even, got_x_even, got_x_odd, got_y_even, got_y_odd, banks, coarse_banks, counts,
    )
    got_both = one_lower(part_both, "gy")
    part_x, part_y = pl.pallas_call(
        sides_kernel,
        out_shape=(shape(VZ * PB, BLK),) * 2,
        in_specs=[IN_VMEM] * 6,
        out_specs=(IN_VMEM,) * 2,
        scratch_shapes=[pltpu.VMEM((2 * NOPS * PB, 2 * CX), BF16), pltpu.VMEM((2, 2 * VZ * PB, NOPS * BLK), BF16)],
        compiler_params=params,
    )(got_x_even, got_x_odd, got_y_even, got_y_odd, fields, banks)
    got_x = one_lower(part_x + got_both, "gx")
    got_y = one_lower(part_y, "gy")
    states, comfort, so_far = pl.pallas_call(
        own_kernel,
        out_shape=(shape(VZ, CX, BLK), shape(CX, BLK), shape(VZ * PB, BLK)),
        in_specs=[IN_VMEM] * 6 + [pl.BlockSpec(memory_space=pl.ANY)],
        out_specs=(IN_HBM, IN_VMEM, IN_VMEM),
        scratch_shapes=select_and_picked + [pltpu.SemaphoreType.DMA],
        compiler_params=params,
    )(x_even, new, fields, banks, radiative_mean_kelvin, parent_slab.reshape(VZ * PB, BLK), part_y)
    parent_new = so_far + 0.5 * (got_y + got_x)
    return states.reshape(child_state.shape), parent_new.reshape(parent_slab.shape), comfort


def solution(mesh):
    placed = (
        P(None, None, "gx", "gy"),
        P(None, None, ("gx", "gy"), None),
        P(None, ("gx", "gy"), None),
        P("gx", "gy"),
        P(),
        P(),
        P(),
        P(None, "gx", "gy"),
        P(("gx", "gy"), None),
        P(("gx", "gy"), None),
        P(("gx", "gy"), None),
        P(),
        P("gx", "gy", None),
        P("gx", "gy", None),
        P("gx", "gy", None),
        P(),
    )
    return jax.shard_map(
        local,
        mesh=mesh,
        in_specs=placed,
        out_specs=(P(None, None, "gx", "gy"), P(None, None, ("gx", "gy"), None), P("gx", "gy")),
        check_vma=False,
    )
```

```python
import jax
import jax.numpy as jnp
from jax import lax
from jax.experimental import pallas as pl
from jax.experimental.pallas import tpu as pltpu
from jax.sharding import PartitionSpec as P

V, NZ, BLK, CX, K, KI, NOPS, PB = 4, 8, 128, 256, 16, 4, 8, 16
VZ = V * NZ
F32, BF16 = jnp.float32, jnp.bfloat16
PAD = 8
CHUNK = 64
EARLY = 2
VMEM_BYTES = 32 * 1024 * 1024

X_ROWS, X_PAR, X_IDX, X_ALL = 0, 64, 128, 144
Y_COLS, Y_PAR, Y_RELAY, Y_IDX, Y_RIDX, Y_ALL = 0, 128, 192, 256, 272, 288

IN_HBM = pl.BlockSpec(memory_space=pltpu.HBM)
IN_VMEM = pl.BlockSpec(memory_space=pltpu.VMEM)
IN_SMEM = pl.BlockSpec(memory_space=pltpu.SMEM)
NT = (((1,), (1,)), ((), ()))
TN = (((0,), (0,)), ((), ()))


def exchange(value, axis, odd):
    pairs = []
    for a in range(odd, lax.axis_size(axis) - 1, 2):
        pairs += [(a, a + 1), (a + 1, a)]
    return lax.ppermute(value, axis, pairs)


def one_lower(value, axis):
    return lax.ppermute(value, axis, [(a, a - 1) for a in range(1, lax.axis_size(axis))])


def split(value):
    high = value.astype(BF16)
    return high, (value - high.astype(F32)).astype(BF16)


def lanes(shape):
    return lax.broadcasted_iota(jnp.int32, shape, len(shape) - 1)


def rows_kernel(child, parent, tile, row, op, even, odd, first, last, blocks, names, stage, sems):
    copies = [
        pltpu.make_async_copy(child.at[:, pl.ds(0, 8)], first, sems.at[0]),
        pltpu.make_async_copy(child.at[:, pl.ds(CX - 8, 8)], last, sems.at[1]),
        pltpu.make_async_copy(parent, blocks, sems.at[2]),
    ] + [pltpu.make_async_copy(a, names.at[i], sems.at[3 + i]) for i, a in enumerate((tile, row, op))]
    for c in copies:
        c.start()
    stage[...] = jnp.zeros_like(stage)
    for c in copies:
        c.wait()
    for i in range(3):
        stage[i, :, 0:K] = names[i].astype(F32)
    index = stage[0] + pltpu.roll(stage[1], K, 1) + pltpu.roll(stage[2], 2 * K, 1)
    flag = lax.axis_index("gx") % 2 == 0
    for buffer in (even, odd):
        buffer[X_PAR:X_IDX] = blocks[...]
        buffer[X_IDX:X_ALL] = index
    for vz in range(VZ):
        low, high = first[vz, 0:2], last[vz, 6:8]
        even[2 * vz : 2 * vz + 2] = jnp.where(flag, high, low)
        odd[2 * vz : 2 * vz + 2] = jnp.where(flag, low, high)


def edges_kernel(courant_x, courant_y, diffusion, child, cells, to_next, to_prev, inner, sems):
    copies = [
        pltpu.make_async_copy(child.at[pl.ds(NZ * v, NZ)], cells.at[pl.ds(NZ * v, NZ), pl.ds(PAD, CX)], sems.at[v])
        for v in range(V)
    ]
    for c in copies:
        c.start()
    for vz in range(VZ):
        cells[vz, 0:PAD] = jnp.zeros((PAD, BLK), F32)
        cells[vz, PAD + CX : PAD + CX + PAD] = jnp.zeros((PAD, BLK), F32)
    which = lanes((CX, BLK)) // 4
    edges = jnp.zeros((CX, BLK), F32)
    for v in range(V):
        copies[v].wait()
        for z in range(NZ):
            vz = NZ * v + z
            edges = jnp.where(which == vz, pltpu.roll(cells[vz, PAD : PAD + CX], (4 * vz + 2) % BLK, 1), edges)
    half = CX // 2
    upper = lanes((half, BLK)) % 4 >= 2
    to_next[...] = jnp.where(upper, pltpu.roll(edges[half:], 2, 1), edges[:half])
    to_prev[...] = jnp.where(upper, edges[:half], pltpu.roll(edges[half:], BLK - 2, 1))
    step_inside(0, EARLY, courant_x, courant_y, diffusion, cells, inner)


def join_kernel(even_x, odd_x, own_even, to_next, to_prev, even, odd):
    flag_x, flag = lax.axis_index("gx") % 2 == 0, lax.axis_index("gy") % 2 == 0
    even[Y_COLS:Y_PAR] = jnp.where(flag, to_next[...], to_prev[...])
    odd[Y_COLS:Y_PAR] = jnp.where(flag, to_prev[...], to_next[...])
    relay = jnp.where(flag_x, odd_x[X_PAR:X_ALL], even_x[X_PAR:X_ALL])
    own = own_even[X_PAR:X_ALL]
    for buffer in (even, odd):
        buffer[Y_PAR:Y_RELAY] = own[:64]
        buffer[Y_RELAY:Y_IDX] = relay[:64]
        buffer[Y_IDX:Y_RIDX] = own[64:]
        buffer[Y_RIDX:Y_ALL] = relay[64:]


def coefficients(courant):
    size = jnp.abs(courant)
    half = 0.5 * size
    return half * size - 1.5 * size, 2.0 * size - size * size, half * size - half


def step_inside(first, last, courant_x, courant_y, diffusion, cells, inner):
    lane = lanes((8, BLK))[0:1]

    def variable(v, carry):
        d = diffusion[v]
        for z in range(NZ):
            sx, sy = courant_x[z], courant_y[z]
            own_x, near_x, far_x = coefficients(sx)
            own_y, near_y, far_y = coefficients(sy)
            up_x, up_y = sx >= 0.0, sy >= 0.0
            own = 1.0 + own_x + own_y - 6.0 * d
            low_x = d + jnp.where(up_x, near_x, 0.0)
            high_x = d + jnp.where(up_x, 0.0, near_x)
            low_far = jnp.where(up_x, far_x, 0.0)
            high_far = jnp.where(up_x, 0.0, far_x)
            low_y = jnp.where(lane == 0, 0.0, d + jnp.where(up_y, near_y, 0.0))
            high_y = jnp.where(lane == BLK - 1, 0.0, d + jnp.where(up_y, 0.0, near_y))
            outside = jnp.where(up_y, 0, BLK - 2)
            far = jnp.where((lane >= outside) & (lane < outside + 2), 0.0, far_y)
            turn_far = jnp.where(up_y, 2, BLK - 2)
            vz = NZ * v + z
            for r in range(PAD, PAD + CX, CHUNK):
                c = cells[vz, r : r + CHUNK]
                total = own * c
                total = total + low_x * cells[vz, r - 1 : r - 1 + CHUNK]
                total = total + high_x * cells[vz, r + 1 : r + 1 + CHUNK]
                total = total + low_far * cells[vz, r - 2 : r - 2 + CHUNK]
                total = total + high_far * cells[vz, r + 2 : r + 2 + CHUNK]
                total = total + low_y * pltpu.roll(c, 1, 1)
                total = total + high_y * pltpu.roll(c, BLK - 1, 1)
                total = total + far * pltpu.roll(c, turn_far, 1)
                beside = None
                if z < NZ - 1:
                    beside = cells[vz + 1, r : r + CHUNK]
                if z > 0:
                    below = cells[vz - 1, r : r + CHUNK]
                    beside = below if beside is None else beside + below
                inner[vz, r - PAD : r - PAD + CHUNK] = total + d * beside
        return carry

    lax.fori_loop(first, last, variable, 0)


def per_level(values, level):
    out = jnp.zeros(level.shape, F32)
    for z in range(NZ):
        out = jnp.where(level == z, values[z], out)
    return out


def choose(names, tile, select, at=0):
    rows = pltpu.roll(names, BLK - K, 1)
    ops = pltpu.roll(names, BLK - 2 * K, 1)
    codes = jnp.where(names == float(tile), ops * float(CX) + rows, -1.0)
    spread = [jnp.broadcast_to(codes[:, k : k + 1], (PB, CX)) for k in range(K)]
    cell = lanes((PB, CX)).astype(F32)
    for o in range(NOPS):
        total = jnp.zeros((PB, CX), F32)
        for k in range(K):
            total = total + jnp.where(spread[k] == cell + float(CX * o), 1.0, 0.0)
        total = total.astype(BF16)
        row = (select.shape[0] // NOPS) * o + PB * at
        select[row : row + PB, 0:CX] = total
        select[row : row + PB, CX : 2 * CX] = total


def gather(select, pair, vz, picked):
    many = select.shape[0] // NOPS
    found = jnp.dot(select[...], pair, preferred_element_type=F32)
    for part, value in enumerate(split(found)):
        for o in range(NOPS):
            for e in range(2):
                picked[part, pl.ds(pl.multiple_of(many * (vz + e), many), many), BLK * o : BLK * (o + 1)] = value[
                    many * o : many * (o + 1), BLK * e : BLK * (e + 1)
                ]


def through_banks(picked, banks):
    both = lax.dot_general(picked[0], banks[...], NT, preferred_element_type=F32)
    rest = lax.dot_general(picked[1], banks[0:BLK], NT, preferred_element_type=F32)
    return both[:, :BLK] + both[:, BLK:] + rest


def gather_all(select, fields, picked):
    def one_pair(i, carry):
        gather(select, fields[:, pl.ds(pl.multiple_of(2 * BLK * i, 2 * BLK), 2 * BLK)], 2 * i, picked)
        return carry

    lax.fori_loop(0, VZ // 2, one_pair, 0, unroll=4)


def ghost_part(blocks, coarse_banks, counts, table):
    high, low = split(jnp.concatenate([blocks[t][PB * v : PB * (v + 1)] for v in range(V) for t in range(2)], axis=0))
    for o in range(NOPS):
        bank_high, bank_low = (coarse_banks[i, BLK * o : BLK * (o + 1)] for i in range(2))
        made = (
            lax.dot_general(high, bank_high, NT, preferred_element_type=F32)
            + lax.dot_general(high, bank_low, NT, preferred_element_type=F32)
            + lax.dot_general(low, bank_high, NT, preferred_element_type=F32)
        )
        made_high, made_low = split(made)
        for v in range(V):
            table[32 * o : 32 * (o + 1), BLK * v : BLK * (v + 1)] = made_high[32 * v : 32 * (v + 1)]
            table[256 + 32 * o : 256 + 32 * (o + 1), BLK * v : BLK * (v + 1)] = made_low[32 * v : 32 * (v + 1)]
    return jnp.dot(counts, table[0:256], preferred_element_type=F32) + jnp.dot(
        counts, table[256:512], preferred_element_type=F32
    )


def middle_kernel(
    courant_x, courant_y, diffusion, so_far, cells, fine, coarse, code, own_x, even_x, odd_x, after,
    inner, banks, coarse_banks, counts_y, ghost, above_fix, below_fix, side_weights, table,
):
    del so_far, after
    flag_x = lax.axis_index("gx") % 2 == 0
    prev_x = jnp.where(flag_x, odd_x[...], even_x[...])

    def weights(courant, level, variable):
        d = jnp.zeros(level.shape, F32)
        for v in range(V):
            d = jnp.where(variable == v, diffusion[v], d)
        s = per_level(courant, level)
        _, near, far = coefficients(s)
        up = s >= 0.0
        return (
            d + jnp.where(up, near, 0.0), d + jnp.where(up, 0.0, near), jnp.where(up, far, 0.0), jnp.where(up, 0.0, far),
        )

    next_rows = jnp.where(flag_x, even_x[X_ROWS:X_PAR], odd_x[X_ROWS:X_PAR])
    prev_rows = prev_x[X_ROWS:X_PAR]
    line = lax.broadcasted_iota(jnp.int32, (2 * VZ, BLK), 0)
    low, high, low_far, high_far = weights(courant_x, (line // 2) % NZ, line // (2 * NZ))
    first = line % 2 == 0
    above_fix[...] = low_far * prev_rows + jnp.where(first, low * pltpu.roll(prev_rows, 2 * VZ - 1, 0), 0.0)
    below_fix[...] = high_far * next_rows + jnp.where(first, 0.0, high * pltpu.roll(next_rows, 1, 0))

    lane = lanes((8, BLK))
    low, high, low_far, high_far = weights(courant_y, (lane // 4) % NZ, lane // (4 * NZ))
    place = lane % 4
    side_weights[0:8] = jnp.where(place < 2, high_far, 0.0)
    side_weights[8:16] = jnp.where(place == 1, high, 0.0)
    side_weights[16:24] = jnp.where(place == 2, low, 0.0)
    side_weights[24:32] = jnp.where(place >= 2, low_far, 0.0)
    for v in range(V):
        side_weights[32 + 8 * v : 40 + 8 * v] = jnp.full((8, BLK), diffusion[v], F32)

    for o in range(NOPS):
        high, low = split(fine[o])
        banks[0:BLK, BLK * o : BLK * (o + 1)] = high
        banks[BLK : 2 * BLK, BLK * o : BLK * (o + 1)] = low
        high, low = split(coarse[o])
        coarse_banks[0, BLK * o : BLK * (o + 1)] = high
        coarse_banks[1, BLK * o : BLK * (o + 1)] = low

    wanted = lax.broadcasted_iota(jnp.int32, (512, CX), 0)
    total = jnp.zeros((512, CX), F32)
    for k in range(KI):
        total = total + jnp.where(code[k : k + 1, :] == wanted, 1.0, 0.0)
    counts_y[...] = total[CX:].T.astype(BF16)
    made = ghost_part([own_x[X_PAR:X_IDX], prev_x[X_PAR:X_IDX]], coarse_banks, total[:CX].T.astype(BF16), table)
    for v in range(V):
        ghost[:, BLK * v : BLK * (v + 1)] = diffusion[v] * made[:, BLK * v : BLK * (v + 1)]
    step_inside(EARLY, V, courant_x, courant_y, diffusion, cells, inner)


def update_kernel(
    inner, walls, even_y, odd_y, banks, coarse_banks, counts_y, ghost_x, above_fix, below_fix, side_weights,
    new, fields, part_both,
    side_fix, select, ghost, table, picked,
):
    flag_y = lax.axis_index("gy") % 2 == 0
    prev_y = jnp.where(flag_y, odd_y[...], even_y[...])

    half = CX // 2
    next_y = jnp.where(flag_y, even_y[Y_COLS:Y_PAR], odd_y[Y_COLS:Y_PAR])
    before = prev_y[Y_COLS:Y_PAR]
    upper = lanes((half, BLK)) % 4 >= 2
    by_minus_2, by_minus_1, by_plus_1, by_plus_2 = (side_weights[8 * i : 8 * i + 1] for i in range(4))
    for part in range(2):
        if part == 0:
            columns = jnp.where(upper, next_y, before)
        else:
            columns = jnp.where(upper, pltpu.roll(next_y, 2, 1), pltpu.roll(before, BLK - 2, 1))
        side_fix[half * part : half * (part + 1)] = (
            by_minus_2 * pltpu.roll(columns, BLK - 2, 1)
            + by_minus_1 * pltpu.roll(columns, BLK - 1, 1)
            + by_plus_1 * pltpu.roll(columns, 1, 1)
            + by_plus_2 * pltpu.roll(columns, 2, 1)
        )

    made = ghost_part([prev_y[Y_PAR:Y_RELAY], prev_y[Y_RELAY:Y_IDX]], coarse_banks, counts_y[...], table)
    for v in range(V):
        at = (slice(None), slice(BLK * v, BLK * (v + 1)))
        ghost[at] = ghost_x[at] + side_weights[32 + 8 * v : 33 + 8 * v] * made[at]

    choose(prev_y[Y_RIDX:Y_ALL], 3, select)
    at_edge = (lanes((CHUNK, BLK)) + 2) % BLK < 4
    no_rows = jnp.zeros((6, BLK), F32)

    def variable(v, carry):
        for z in range(NZ):
            vz = NZ * v + z
            turn = (2 * BLK - 2 - 4 * vz) % BLK
            for r in range(0, CX, CHUNK):
                total = inner[vz, r : r + CHUNK]
                total = total + jnp.where(at_edge, pltpu.roll(side_fix[r : r + CHUNK], turn, 1), 0.0)
                if z == NZ - 1:
                    total = total + ghost[r : r + CHUNK, pl.ds(pl.multiple_of(BLK * v, BLK), BLK)]
                if r == 0:
                    fix = jnp.concatenate([above_fix[pl.ds(2 * vz, 2)], no_rows], axis=0)
                    total = jnp.concatenate([total[:8] + fix, total[8:]], axis=0)
                if r == CX - CHUNK:
                    fix = jnp.concatenate([no_rows, below_fix[pl.ds(2 * vz, 2)]], axis=0)
                    total = jnp.concatenate([total[:-8], total[-8:] + fix], axis=0)
                total = jnp.where(walls[z, r : r + CHUNK] == 1, 0.0, total)
                new[vz, r : r + CHUNK] = total
                high, low = split(total)
                columns = pl.ds(pl.multiple_of(BLK * vz, BLK), BLK)
                fields[r : r + CHUNK, columns] = high
                fields[CX + r : CX + r + CHUNK, columns] = low
            if z % 2 == 1:
                pair = pl.ds(pl.multiple_of(BLK * (vz - 1), BLK), 2 * BLK)
                gather(select, fields[:, pair], vz - 1, picked)
        return carry

    lax.fori_loop(0, V, variable, 0)
    part_both[...] = through_banks(picked, banks)


def sides_kernel(even_x, odd_x, even_y, odd_y, fields, banks, part_x, part_y, select, picked):
    flag_x, flag_y = lax.axis_index("gx") % 2 == 0, lax.axis_index("gy") % 2 == 0
    choose(jnp.where(flag_x, odd_x[X_IDX:X_ALL], even_x[X_IDX:X_ALL]), 1, select, 0)
    choose(jnp.where(flag_y, odd_y[Y_IDX:Y_RIDX], even_y[Y_IDX:Y_RIDX]), 2, select, 1)
    gather_all(select, fields, picked)
    result = through_banks(picked, banks)
    for vz in range(VZ):
        part_x[PB * vz : PB * (vz + 1)] = result[2 * PB * vz : 2 * PB * vz + PB]
        part_y[PB * vz : PB * (vz + 1)] = result[2 * PB * vz + PB : 2 * PB * (vz + 1)]


def add_kernel(part_x, got_both, part_y, to_x, to_y):
    to_x[...] = part_x[...] + got_both[...]
    to_y[...] = part_y[...]


def own_kernel(own_x, new, fields, banks, radiant, slab, after, states, comfort, so_far, select, picked, sem):
    del after
    out = pltpu.make_async_copy(new, states, sem)
    out.start()
    choose(own_x[X_IDX:X_ALL], 0, select)
    gather_all(select, fields, picked)
    so_far[...] = 0.5 * slab[...] + 0.5 * through_banks(picked, banks)
    u, w, t, h = (new[NZ * v] for v in range(V))
    speed = jnp.sqrt(u * u + w * w + 0.25)
    excess = radiant[...] - t
    comfort[...] = t + 0.3 * excess - 0.6 * (speed - 1.0) + 0.4 * h + 0.1 * t * excess - 0.15 * speed * excess
    out.wait()


def shape(*dims, kind=F32):
    return jax.ShapeDtypeStruct(dims, kind)


def local(
    child_state, parent_slab, parent_above, radiative_mean_kelvin, courant_x, courant_y, diffusion, building,
    fine_tile, fine_row, fine_op, fine_bank, coarse_tile, coarse_row, coarse_op, coarse_bank,
):
    child = child_state.reshape(VZ, CX, BLK)
    parent = parent_above.reshape(V * PB, BLK)
    params = pltpu.CompilerParams(vmem_limit_bytes=VMEM_BYTES)
    x_even, x_odd = pl.pallas_call(
        rows_kernel,
        out_shape=(shape(X_ALL, BLK), shape(X_ALL, BLK)),
        in_specs=[IN_HBM] * 5,
        out_specs=(IN_VMEM,) * 2,
        scratch_shapes=[
            pltpu.VMEM((VZ, 8, BLK), F32), pltpu.VMEM((VZ, 8, BLK), F32), pltpu.VMEM((V * PB, BLK), F32),
            pltpu.VMEM((3, PB, K), jnp.int32), pltpu.VMEM((3, PB, BLK), F32), pltpu.SemaphoreType.DMA((6,)),
        ],
        compiler_params=pltpu.CompilerParams(vmem_limit_bytes=56 * 1024 * 1024),
    )(child, parent, fine_tile, fine_row, fine_op)
    got_x_even = exchange(x_even, "gx", 0)
    got_x_odd = exchange(x_odd, "gx", 1)
    coarse_code = ((coarse_tile >> 1) * 256 + coarse_op * 32 + (coarse_tile & 1) * PB + coarse_row).reshape(CX, KI).T
    cells, to_next, to_prev, inner = pl.pallas_call(
        edges_kernel,
        out_shape=(
            shape(VZ, CX + 2 * PAD, BLK), shape(CX // 2, BLK), shape(CX // 2, BLK), shape(VZ, CX, BLK),
        ),
        in_specs=[IN_SMEM] * 3 + [IN_HBM],
        out_specs=(IN_VMEM,) * 4,
        scratch_shapes=[pltpu.SemaphoreType.DMA((V,))],
        compiler_params=params,
    )(courant_x, courant_y, diffusion, child)
    y_even, y_odd = pl.pallas_call(
        join_kernel,
        out_shape=(shape(Y_ALL, BLK), shape(Y_ALL, BLK)),
        in_specs=[IN_VMEM] * 5,
        out_specs=(IN_VMEM,) * 2,
        compiler_params=params,
    )(got_x_even, got_x_odd, x_even, to_next, to_prev)
    got_y_odd = exchange(y_odd, "gy", 1)
    got_y_even = exchange(y_even, "gy", 0)
    inner, banks, coarse_banks, counts_y, ghost, above_fix, below_fix, side_weights = pl.pallas_call(
        middle_kernel,
        out_shape=(
            shape(VZ, CX, BLK), shape(2 * BLK, NOPS * BLK, kind=BF16), shape(2, NOPS * BLK, BLK, kind=BF16),
            shape(CX, CX, kind=BF16), shape(CX, V * BLK), shape(2 * VZ, BLK), shape(2 * VZ, BLK), shape(64, BLK),
        ),
        in_specs=[IN_SMEM] * 3 + [IN_VMEM] * 8 + [pl.BlockSpec(memory_space=pl.ANY)],
        out_specs=(IN_VMEM,) * 8,
        input_output_aliases={3: 0},
        scratch_shapes=[pltpu.VMEM((512, V * BLK), BF16)],
        compiler_params=params,
    )(
        courant_x, courant_y, diffusion, inner, cells, fine_bank, coarse_bank, coarse_code, x_even, got_x_even, got_x_odd,
        y_even,
    )
    fields_shape = shape(2 * CX, VZ * BLK, kind=BF16)
    select_and_picked = [pltpu.VMEM((NOPS * PB, 2 * CX), BF16), pltpu.VMEM((2, VZ * PB, NOPS * BLK), BF16)]
    new, fields, part_both = pl.pallas_call(
        update_kernel,
        out_shape=(shape(VZ, CX, BLK), fields_shape, shape(VZ * PB, BLK)),
        in_specs=[IN_VMEM] * 11,
        out_specs=(IN_VMEM,) * 3,
        input_output_aliases={0: 0},
        scratch_shapes=[
            pltpu.VMEM((CX, BLK), F32),
            select_and_picked[0],
            pltpu.VMEM((CX, V * BLK), F32),
            pltpu.VMEM((512, V * BLK), BF16),
            select_and_picked[1],
        ],
        compiler_params=params,
    )(
        inner, building, got_y_even, got_y_odd, banks, coarse_banks, counts_y, ghost, above_fix, below_fix, side_weights,
    )
    got_both = one_lower(part_both, "gy")
    part_x, part_y = pl.pallas_call(
        sides_kernel,
        out_shape=(shape(VZ * PB, BLK),) * 2,
        in_specs=[IN_VMEM] * 6,
        out_specs=(IN_VMEM,) * 2,
        scratch_shapes=[pltpu.VMEM((2 * NOPS * PB, 2 * CX), BF16), pltpu.VMEM((2, 2 * VZ * PB, NOPS * BLK), BF16)],
        compiler_params=params,
    )(got_x_even, got_x_odd, got_y_even, got_y_odd, fields, banks)
    got_x = one_lower(part_x + got_both, "gx")
    got_y = one_lower(part_y, "gy")
    states, comfort, so_far = pl.pallas_call(
        own_kernel,
        out_shape=(shape(VZ, CX, BLK), shape(CX, BLK), shape(VZ * PB, BLK)),
        in_specs=[IN_VMEM] * 6 + [pl.BlockSpec(memory_space=pl.ANY)],
        out_specs=(IN_HBM, IN_VMEM, IN_VMEM),
        scratch_shapes=select_and_picked + [pltpu.SemaphoreType.DMA],
        compiler_params=params,
    )(x_even, new, fields, banks, radiative_mean_kelvin, parent_slab.reshape(VZ * PB, BLK), part_y)
    parent_new = so_far + 0.5 * (got_y + got_x)
    return states.reshape(child_state.shape), parent_new.reshape(parent_slab.shape), comfort


def solution(mesh):
    placed = (
        P(None, None, "gx", "gy"),
        P(None, None, ("gx", "gy"), None),
        P(None, ("gx", "gy"), None),
        P("gx", "gy"),
        P(),
        P(),
        P(),
        P(None, "gx", "gy"),
        P(("gx", "gy"), None),
        P(("gx", "gy"), None),
        P(("gx", "gy"), None),
        P(),
        P("gx", "gy", None),
        P("gx", "gy", None),
        P("gx", "gy", None),
        P(),
    )
    return jax.shard_map(
        local,
        mesh=mesh,
        in_specs=placed,
        out_specs=(P(None, None, "gx", "gy"), P(None, None, ("gx", "gy"), None), P("gx", "gy")),
        check_vma=False,
    )
```

```python
import jax
import jax.numpy as jnp
from jax import lax
from jax.experimental import pallas as pl
from jax.experimental.pallas import tpu as pltpu
from jax.sharding import PartitionSpec as P

V, NZ, BLK, CX, K, KI, NOPS, PB = 4, 8, 128, 256, 16, 4, 8, 16
VZ = V * NZ
F32, BF16 = jnp.float32, jnp.bfloat16
PAD = 8
CHUNK = 64
EARLY = 3
VMEM_BYTES = 32 * 1024 * 1024

X_ROWS, X_PAR, X_IDX, X_ALL = 0, 64, 128, 144
Y_COLS, Y_PAR, Y_RELAY, Y_IDX, Y_RIDX, Y_ALL = 0, 128, 192, 256, 272, 288

IN_HBM = pl.BlockSpec(memory_space=pltpu.HBM)
IN_VMEM = pl.BlockSpec(memory_space=pltpu.VMEM)
IN_SMEM = pl.BlockSpec(memory_space=pltpu.SMEM)
NT = (((1,), (1,)), ((), ()))
TN = (((0,), (0,)), ((), ()))


def exchange(value, axis, odd):
    pairs = []
    for a in range(odd, lax.axis_size(axis) - 1, 2):
        pairs += [(a, a + 1), (a + 1, a)]
    return lax.ppermute(value, axis, pairs)


def one_lower(value, axis):
    return lax.ppermute(value, axis, [(a, a - 1) for a in range(1, lax.axis_size(axis))])


def split(value):
    high = value.astype(BF16)
    return high, (value - high.astype(F32)).astype(BF16)


def lanes(shape):
    return lax.broadcasted_iota(jnp.int32, shape, len(shape) - 1)


def rows_kernel(child, parent, tile, row, op, even, odd, first, last, blocks, names, stage, sems):
    copies = [
        pltpu.make_async_copy(child.at[:, pl.ds(0, 8)], first, sems.at[0]),
        pltpu.make_async_copy(child.at[:, pl.ds(CX - 8, 8)], last, sems.at[1]),
        pltpu.make_async_copy(parent, blocks, sems.at[2]),
    ] + [pltpu.make_async_copy(a, names.at[i], sems.at[3 + i]) for i, a in enumerate((tile, row, op))]
    for c in copies:
        c.start()
    stage[...] = jnp.zeros_like(stage)
    for c in copies:
        c.wait()
    for i in range(3):
        stage[i, :, 0:K] = names[i].astype(F32)
    index = stage[0] + pltpu.roll(stage[1], K, 1) + pltpu.roll(stage[2], 2 * K, 1)
    flag = lax.axis_index("gx") % 2 == 0
    for buffer in (even, odd):
        buffer[X_PAR:X_IDX] = blocks[...]
        buffer[X_IDX:X_ALL] = index
    for vz in range(VZ):
        low, high = first[vz, 0:2], last[vz, 6:8]
        even[2 * vz : 2 * vz + 2] = jnp.where(flag, high, low)
        odd[2 * vz : 2 * vz + 2] = jnp.where(flag, low, high)


def edges_kernel(courant_x, courant_y, diffusion, child, cells, to_next, to_prev, inner, sems):
    copies = [
        pltpu.make_async_copy(child.at[pl.ds(NZ * v, NZ)], cells.at[pl.ds(NZ * v, NZ), pl.ds(PAD, CX)], sems.at[v])
        for v in range(V)
    ]
    for c in copies:
        c.start()
    for vz in range(VZ):
        cells[vz, 0:PAD] = jnp.zeros((PAD, BLK), F32)
        cells[vz, PAD + CX : PAD + CX + PAD] = jnp.zeros((PAD, BLK), F32)
    which = lanes((CX, BLK)) // 4
    edges = jnp.zeros((CX, BLK), F32)
    for v in range(V):
        copies[v].wait()
        for z in range(NZ):
            vz = NZ * v + z
            edges = jnp.where(which == vz, pltpu.roll(cells[vz, PAD : PAD + CX], (4 * vz + 2) % BLK, 1), edges)
    half = CX // 2
    upper = lanes((half, BLK)) % 4 >= 2
    to_next[...] = jnp.where(upper, pltpu.roll(edges[half:], 2, 1), edges[:half])
    to_prev[...] = jnp.where(upper, edges[:half], pltpu.roll(edges[half:], BLK - 2, 1))
    step_inside(0, EARLY, courant_x, courant_y, diffusion, cells, inner)


def join_kernel(even_x, odd_x, own_even, to_next, to_prev, even, odd):
    flag_x, flag = lax.axis_index("gx") % 2 == 0, lax.axis_index("gy") % 2 == 0
    even[Y_COLS:Y_PAR] = jnp.where(flag, to_next[...], to_prev[...])
    odd[Y_COLS:Y_PAR] = jnp.where(flag, to_prev[...], to_next[...])
    relay = jnp.where(flag_x, odd_x[X_PAR:X_ALL], even_x[X_PAR:X_ALL])
    own = own_even[X_PAR:X_ALL]
    for buffer in (even, odd):
        buffer[Y_PAR:Y_RELAY] = own[:64]
        buffer[Y_RELAY:Y_IDX] = relay[:64]
        buffer[Y_IDX:Y_RIDX] = own[64:]
        buffer[Y_RIDX:Y_ALL] = relay[64:]


def coefficients(courant):
    size = jnp.abs(courant)
    half = 0.5 * size
    return half * size - 1.5 * size, 2.0 * size - size * size, half * size - half


def step_inside(first, last, courant_x, courant_y, diffusion, cells, inner):
    lane = lanes((8, BLK))[0:1]

    def variable(v, carry):
        d = diffusion[v]
        for z in range(NZ):
            sx, sy = courant_x[z], courant_y[z]
            own_x, near_x, far_x = coefficients(sx)
            own_y, near_y, far_y = coefficients(sy)
            up_x, up_y = sx >= 0.0, sy >= 0.0
            own = 1.0 + own_x + own_y - 6.0 * d
            low_x = d + jnp.where(up_x, near_x, 0.0)
            high_x = d + jnp.where(up_x, 0.0, near_x)
            low_far = jnp.where(up_x, far_x, 0.0)
            high_far = jnp.where(up_x, 0.0, far_x)
            low_y = jnp.where(lane == 0, 0.0, d + jnp.where(up_y, near_y, 0.0))
            high_y = jnp.where(lane == BLK - 1, 0.0, d + jnp.where(up_y, 0.0, near_y))
            outside = jnp.where(up_y, 0, BLK - 2)
            far = jnp.where((lane >= outside) & (lane < outside + 2), 0.0, far_y)
            turn_far = jnp.where(up_y, 2, BLK - 2)
            vz = NZ * v + z
            for r in range(PAD, PAD + CX, CHUNK):
                c = cells[vz, r : r + CHUNK]
                total = own * c
                total = total + low_x * cells[vz, r - 1 : r - 1 + CHUNK]
                total = total + high_x * cells[vz, r + 1 : r + 1 + CHUNK]
                total = total + low_far * cells[vz, r - 2 : r - 2 + CHUNK]
                total = total + high_far * cells[vz, r + 2 : r + 2 + CHUNK]
                total = total + low_y * pltpu.roll(c, 1, 1)
                total = total + high_y * pltpu.roll(c, BLK - 1, 1)
                total = total + far * pltpu.roll(c, turn_far, 1)
                beside = None
                if z < NZ - 1:
                    beside = cells[vz + 1, r : r + CHUNK]
                if z > 0:
                    below = cells[vz - 1, r : r + CHUNK]
                    beside = below if beside is None else beside + below
                inner[vz, r - PAD : r - PAD + CHUNK] = total + d * beside
        return carry

    lax.fori_loop(first, last, variable, 0)


def per_level(values, level):
    out = jnp.zeros(level.shape, F32)
    for z in range(NZ):
        out = jnp.where(level == z, values[z], out)
    return out


def choose(names, tile, select, at=0):
    rows = pltpu.roll(names, BLK - K, 1)
    ops = pltpu.roll(names, BLK - 2 * K, 1)
    codes = jnp.where(names == float(tile), ops * float(CX) + rows, -1.0)
    spread = [jnp.broadcast_to(codes[:, k : k + 1], (PB, CX)) for k in range(K)]
    cell = lanes((PB, CX)).astype(F32)
    for o in range(NOPS):
        total = jnp.zeros((PB, CX), F32)
        for k in range(K):
            total = total + jnp.where(spread[k] == cell + float(CX * o), 1.0, 0.0)
        total = total.astype(BF16)
        row = (select.shape[0] // NOPS) * o + PB * at
        select[row : row + PB, 0:CX] = total
        select[row : row + PB, CX : 2 * CX] = total


def turn_of(vz):
    return (2 * BLK - 2 - 4 * vz) % BLK


def at_edges(rows):
    return (lanes((rows, BLK)) + 2) % BLK < 4


def through_banks(picked, banks):
    both = lax.dot_general(picked[0], banks[...], NT, preferred_element_type=F32)
    rest = lax.dot_general(picked[1], banks[0:BLK], NT, preferred_element_type=F32)
    return both[:, :BLK] + both[:, BLK:] + rest


def gather_all(select, fields, side, edge, picked):
    rows = select.shape[0]
    many = rows // NOPS
    edge[...] = jnp.dot(select[...], side[...], preferred_element_type=F32)
    near = at_edges(rows)

    def one_pair(i, carry):
        pair = fields[:, pl.ds(pl.multiple_of(2 * BLK * i, 2 * BLK), 2 * BLK)]
        found = jnp.dot(select[...], pair, preferred_element_type=F32)
        for e in range(2):
            vz = 2 * i + e
            whole = found[:, BLK * e : BLK * (e + 1)] + jnp.where(near, pltpu.roll(edge[...], turn_of(vz), 1), 0.0)
            for part, value in enumerate(split(whole)):
                for o in range(NOPS):
                    picked[part, pl.ds(pl.multiple_of(many * vz, many), many), BLK * o : BLK * (o + 1)] = value[
                        many * o : many * (o + 1)
                    ]
        return carry

    lax.fori_loop(0, VZ // 2, one_pair, 0, unroll=4)


def ghost_part(blocks, coarse_banks, counts, table):
    high, low = split(jnp.concatenate([blocks[t][PB * v : PB * (v + 1)] for v in range(V) for t in range(2)], axis=0))
    for o in range(NOPS):
        bank_high, bank_low = (coarse_banks[i, BLK * o : BLK * (o + 1)] for i in range(2))
        made = (
            lax.dot_general(high, bank_high, NT, preferred_element_type=F32)
            + lax.dot_general(high, bank_low, NT, preferred_element_type=F32)
            + lax.dot_general(low, bank_high, NT, preferred_element_type=F32)
        )
        made_high, made_low = split(made)
        for v in range(V):
            table[32 * o : 32 * (o + 1), BLK * v : BLK * (v + 1)] = made_high[32 * v : 32 * (v + 1)]
            table[256 + 32 * o : 256 + 32 * (o + 1), BLK * v : BLK * (v + 1)] = made_low[32 * v : 32 * (v + 1)]
    return jnp.dot(counts, table[0:256], preferred_element_type=F32) + jnp.dot(
        counts, table[256:512], preferred_element_type=F32
    )


def middle_kernel(
    courant_x, courant_y, diffusion, so_far, cells, walls, fine, coarse, code, own_x, even_x, odd_x, after,
    inner, fields, banks, coarse_banks, counts_y, side_weights, open_sides, ghost, above_fix, below_fix, table,
):
    del so_far, after
    flag_x = lax.axis_index("gx") % 2 == 0
    prev_x = jnp.where(flag_x, odd_x[...], even_x[...])

    def weights(courant, level, variable):
        d = jnp.zeros(level.shape, F32)
        for v in range(V):
            d = jnp.where(variable == v, diffusion[v], d)
        s = per_level(courant, level)
        _, near, far = coefficients(s)
        up = s >= 0.0
        return (
            d + jnp.where(up, near, 0.0), d + jnp.where(up, 0.0, near), jnp.where(up, far, 0.0), jnp.where(up, 0.0, far),
        )

    next_rows = jnp.where(flag_x, even_x[X_ROWS:X_PAR], odd_x[X_ROWS:X_PAR])
    prev_rows = prev_x[X_ROWS:X_PAR]
    line = lax.broadcasted_iota(jnp.int32, (2 * VZ, BLK), 0)
    low, high, low_far, high_far = weights(courant_x, (line // 2) % NZ, line // (2 * NZ))
    first = line % 2 == 0
    above_fix[...] = low_far * prev_rows + jnp.where(first, low * pltpu.roll(prev_rows, 2 * VZ - 1, 0), 0.0)
    below_fix[...] = high_far * next_rows + jnp.where(first, 0.0, high * pltpu.roll(next_rows, 1, 0))

    lane = lanes((8, BLK))
    low, high, low_far, high_far = weights(courant_y, (lane // 4) % NZ, lane // (4 * NZ))
    place = lane % 4
    side_weights[0:8] = jnp.where(place < 2, high_far, 0.0)
    side_weights[8:16] = jnp.where(place == 1, high, 0.0)
    side_weights[16:24] = jnp.where(place == 2, low, 0.0)
    side_weights[24:32] = jnp.where(place >= 2, low_far, 0.0)
    for v in range(V):
        side_weights[32 + 8 * v : 40 + 8 * v] = jnp.full((8, BLK), diffusion[v], F32)

    for o in range(NOPS):
        high, low = split(fine[o])
        banks[0:BLK, BLK * o : BLK * (o + 1)] = high
        banks[BLK : 2 * BLK, BLK * o : BLK * (o + 1)] = low
        high, low = split(coarse[o])
        coarse_banks[0, BLK * o : BLK * (o + 1)] = high
        coarse_banks[1, BLK * o : BLK * (o + 1)] = low

    wanted = lax.broadcasted_iota(jnp.int32, (512, CX), 0)
    total = jnp.zeros((512, CX), F32)
    for k in range(KI):
        total = total + jnp.where(code[k : k + 1, :] == wanted, 1.0, 0.0)
    counts_y[...] = total[CX:].T.astype(BF16)
    made = ghost_part([own_x[X_PAR:X_IDX], prev_x[X_PAR:X_IDX]], coarse_banks, total[:CX].T.astype(BF16), table)
    for v in range(V):
        ghost[:, BLK * v : BLK * (v + 1)] = diffusion[v] * made[:, BLK * v : BLK * (v + 1)]
    step_inside(EARLY, V, courant_x, courant_y, diffusion, cells, inner)

    for r in range(0, CX, CHUNK):
        level = lanes((CHUNK, BLK)) // 4
        marks = jnp.zeros((CHUNK, BLK), F32)
        for z in range(NZ):
            wall = jnp.where(walls[z, r : r + CHUNK] == 1, 0.0, 1.0)
            marks = jnp.where(level == z, pltpu.roll(wall, 4 * z + 2, 1), marks)
        total = marks
        for v in range(1, V):
            total = total + pltpu.roll(marks, 4 * NZ * v, 1)
        open_sides[r : r + CHUNK] = total

    no_rows = jnp.zeros((6, BLK), F32)

    def variable(v, carry):
        for z in range(NZ):
            vz = NZ * v + z
            for r in range(0, CX, CHUNK):
                total = inner[vz, r : r + CHUNK]
                if z == NZ - 1:
                    total = total + ghost[r : r + CHUNK, pl.ds(pl.multiple_of(BLK * v, BLK), BLK)]
                if r == 0:
                    fix = jnp.concatenate([above_fix[pl.ds(2 * vz, 2)], no_rows], axis=0)
                    total = jnp.concatenate([total[:8] + fix, total[8:]], axis=0)
                if r == CX - CHUNK:
                    fix = jnp.concatenate([no_rows, below_fix[pl.ds(2 * vz, 2)]], axis=0)
                    total = jnp.concatenate([total[:-8], total[-8:] + fix], axis=0)
                total = jnp.where(walls[z, r : r + CHUNK] == 1, 0.0, total)
                inner[vz, r : r + CHUNK] = total
                high, low = split(total)
                columns = pl.ds(pl.multiple_of(BLK * vz, BLK), BLK)
                fields[r : r + CHUNK, columns] = high
                fields[CX + r : CX + r + CHUNK, columns] = low
        return carry

    lax.fori_loop(0, V, variable, 0)


def update_kernel(
    old, old_fields, walls, even_y, odd_y, banks, coarse_banks, counts_y, side_weights, open_sides,
    new, fields, side_fix, side, part_both,
    select, edge, table, picked,
):
    del old, old_fields
    flag_y = lax.axis_index("gy") % 2 == 0
    prev_y = jnp.where(flag_y, odd_y[...], even_y[...])

    half = CX // 2
    next_y = jnp.where(flag_y, even_y[Y_COLS:Y_PAR], odd_y[Y_COLS:Y_PAR])
    before = prev_y[Y_COLS:Y_PAR]
    upper = lanes((half, BLK)) % 4 >= 2
    by_minus_2, by_minus_1, by_plus_1, by_plus_2 = (side_weights[8 * i : 8 * i + 1] for i in range(4))
    for part in range(2):
        at = slice(half * part, half * (part + 1))
        if part == 0:
            columns = jnp.where(upper, next_y, before)
        else:
            columns = jnp.where(upper, pltpu.roll(next_y, 2, 1), pltpu.roll(before, BLK - 2, 1))
        total = (
            by_minus_2 * pltpu.roll(columns, BLK - 2, 1)
            + by_minus_1 * pltpu.roll(columns, BLK - 1, 1)
            + by_plus_1 * pltpu.roll(columns, 1, 1)
            + by_plus_2 * pltpu.roll(columns, 2, 1)
        )
        total = jnp.where(open_sides[at] > 0.5, total, 0.0)
        side_fix[at] = total
        side[at], side[CX + half * part : CX + half * (part + 1)] = split(total)

    made = ghost_part([prev_y[Y_PAR:Y_RELAY], prev_y[Y_RELAY:Y_IDX]], coarse_banks, counts_y[...], table)
    for v in range(V):
        vz = NZ * v + NZ - 1
        added = side_weights[32 + 8 * v : 33 + 8 * v] * made[:, BLK * v : BLK * (v + 1)]
        total = new[vz] + jnp.where(walls[NZ - 1] == 1, 0.0, added)
        new[vz] = total
        columns = slice(BLK * vz, BLK * (vz + 1))
        fields[0:CX, columns], fields[CX : 2 * CX, columns] = split(total)

    choose(prev_y[Y_RIDX:Y_ALL], 3, select)
    gather_all(select, fields, side, edge, picked)
    part_both[...] = through_banks(picked, banks)


def sides_kernel(even_x, odd_x, even_y, odd_y, fields, side, banks, part_x, part_y, select, edge, picked):
    flag_x, flag_y = lax.axis_index("gx") % 2 == 0, lax.axis_index("gy") % 2 == 0
    choose(jnp.where(flag_x, odd_x[X_IDX:X_ALL], even_x[X_IDX:X_ALL]), 1, select, 0)
    choose(jnp.where(flag_y, odd_y[Y_IDX:Y_RIDX], even_y[Y_IDX:Y_RIDX]), 2, select, 1)
    gather_all(select, fields, side, edge, picked)
    result = through_banks(picked, banks)
    for vz in range(VZ):
        part_x[PB * vz : PB * (vz + 1)] = result[2 * PB * vz : 2 * PB * vz + PB]
        part_y[PB * vz : PB * (vz + 1)] = result[2 * PB * vz + PB : 2 * PB * (vz + 1)]


def add_kernel(part_x, got_both, part_y, to_x, to_y):
    to_x[...] = part_x[...] + got_both[...]
    to_y[...] = part_y[...]


def own_kernel(
    own_x, new, side_fix, fields, side, banks, radiant, slab, after,
    states, comfort, so_far,
    whole, select, edge, picked, sems,
):
    del after
    near = at_edges(CHUNK)

    def variable(v, carry):
        for z in range(NZ):
            vz = NZ * v + z
            for r in range(0, CX, CHUNK):
                turned = pltpu.roll(side_fix[r : r + CHUNK], turn_of(vz), 1)
                whole[vz, r : r + CHUNK] = new[vz, r : r + CHUNK] + jnp.where(near, turned, 0.0)
        pltpu.make_async_copy(whole.at[pl.ds(NZ * v, NZ)], states.at[pl.ds(NZ * v, NZ)], sems.at[v]).start()
        return carry

    lax.fori_loop(0, V, variable, 0)
    u, w, t, h = (whole[NZ * v] for v in range(V))
    speed = jnp.sqrt(u * u + w * w + 0.25)
    excess = radiant[...] - t
    comfort[...] = t + 0.3 * excess - 0.6 * (speed - 1.0) + 0.4 * h + 0.1 * t * excess - 0.15 * speed * excess
    choose(own_x[X_IDX:X_ALL], 0, select)
    gather_all(select, fields, side, edge, picked)
    so_far[...] = 0.5 * slab[...] + 0.5 * through_banks(picked, banks)
    for v in range(V):
        pltpu.make_async_copy(whole.at[pl.ds(NZ * v, NZ)], states.at[pl.ds(NZ * v, NZ)], sems.at[v]).wait()


def shape(*dims, kind=F32):
    return jax.ShapeDtypeStruct(dims, kind)


def local(
    child_state, parent_slab, parent_above, radiative_mean_kelvin, courant_x, courant_y, diffusion, building,
    fine_tile, fine_row, fine_op, fine_bank, coarse_tile, coarse_row, coarse_op, coarse_bank,
):
    child = child_state.reshape(VZ, CX, BLK)
    parent = parent_above.reshape(V * PB, BLK)
    params = pltpu.CompilerParams(vmem_limit_bytes=VMEM_BYTES)
    x_even, x_odd = pl.pallas_call(
        rows_kernel,
        out_shape=(shape(X_ALL, BLK), shape(X_ALL, BLK)),
        in_specs=[IN_HBM] * 5,
        out_specs=(IN_VMEM,) * 2,
        scratch_shapes=[
            pltpu.VMEM((VZ, 8, BLK), F32), pltpu.VMEM((VZ, 8, BLK), F32), pltpu.VMEM((V * PB, BLK), F32),
            pltpu.VMEM((3, PB, K), jnp.int32), pltpu.VMEM((3, PB, BLK), F32), pltpu.SemaphoreType.DMA((6,)),
        ],
        compiler_params=params,
    )(*(pltpu.with_memory_space_constraint(a, pltpu.HBM) for a in (child, parent, fine_tile, fine_row, fine_op)))
    got_x_even = exchange(x_even, "gx", 0)
    got_x_odd = exchange(x_odd, "gx", 1)
    coarse_code = ((coarse_tile >> 1) * 256 + coarse_op * 32 + (coarse_tile & 1) * PB + coarse_row).reshape(CX, KI).T
    cells, to_next, to_prev, inner = pl.pallas_call(
        edges_kernel,
        out_shape=(
            shape(VZ, CX + 2 * PAD, BLK), shape(CX // 2, BLK), shape(CX // 2, BLK), shape(VZ, CX, BLK),
        ),
        in_specs=[IN_SMEM] * 3 + [IN_HBM],
        out_specs=(IN_VMEM,) * 4,
        scratch_shapes=[pltpu.SemaphoreType.DMA((V,))],
        compiler_params=params,
    )(courant_x, courant_y, diffusion, child)
    y_even, y_odd = pl.pallas_call(
        join_kernel,
        out_shape=(shape(Y_ALL, BLK), shape(Y_ALL, BLK)),
        in_specs=[IN_VMEM] * 5,
        out_specs=(IN_VMEM,) * 2,
        compiler_params=params,
    )(got_x_even, got_x_odd, x_even, to_next, to_prev)
    got_y_odd = exchange(y_odd, "gy", 1)
    got_y_even = exchange(y_even, "gy", 0)
    fields_shape = shape(2 * CX, VZ * BLK, kind=BF16)
    inner, fields, banks, coarse_banks, counts_y, side_weights, open_sides = pl.pallas_call(
        middle_kernel,
        out_shape=(
            shape(VZ, CX, BLK), fields_shape, shape(2 * BLK, NOPS * BLK, kind=BF16), shape(2, NOPS * BLK, BLK, kind=BF16),
            shape(CX, CX, kind=BF16), shape(64, BLK), shape(CX, BLK),
        ),
        in_specs=[IN_SMEM] * 3 + [IN_VMEM] * 9 + [pl.BlockSpec(memory_space=pl.ANY)],
        out_specs=(IN_VMEM,) * 7,
        input_output_aliases={3: 0},
        scratch_shapes=[
            pltpu.VMEM((CX, V * BLK), F32),
            pltpu.VMEM((2 * VZ, BLK), F32),
            pltpu.VMEM((2 * VZ, BLK), F32),
            pltpu.VMEM((512, V * BLK), BF16),
        ],
        compiler_params=params,
    )(
        courant_x, courant_y, diffusion, inner, cells, building, fine_bank, coarse_bank, coarse_code,
        x_even, got_x_even, got_x_odd, y_even,
    )

    def choosing(tiles):
        rows = tiles * NOPS * PB
        return [
            pltpu.VMEM((rows, 2 * CX), BF16),
            pltpu.VMEM((rows, BLK), F32),
        ]

    new, fields, side_fix, side, part_both = pl.pallas_call(
        update_kernel,
        out_shape=(
            shape(VZ, CX, BLK), fields_shape, shape(CX, BLK), shape(2 * CX, BLK, kind=BF16), shape(VZ * PB, BLK),
        ),
        in_specs=[IN_VMEM] * 10,
        out_specs=(IN_VMEM,) * 5,
        input_output_aliases={0: 0, 1: 1},
        scratch_shapes=choosing(1) + [
            pltpu.VMEM((512, V * BLK), BF16),
            pltpu.VMEM((2, VZ * PB, NOPS * BLK), BF16),
        ],
        compiler_params=params,
    )(inner, fields, building, got_y_even, got_y_odd, banks, coarse_banks, counts_y, side_weights, open_sides)
    got_both = one_lower(part_both, "gy")
    part_x, part_y = pl.pallas_call(
        sides_kernel,
        out_shape=(shape(VZ * PB, BLK),) * 2,
        in_specs=[IN_VMEM] * 7,
        out_specs=(IN_VMEM,) * 2,
        scratch_shapes=choosing(2) + [pltpu.VMEM((2, 2 * VZ * PB, NOPS * BLK), BF16)],
        compiler_params=params,
    )(got_x_even, got_x_odd, got_y_even, got_y_odd, fields, side, banks)
    got_x = one_lower(part_x + got_both, "gx")
    got_y = one_lower(part_y, "gy")
    states, comfort, so_far = pl.pallas_call(
        own_kernel,
        out_shape=(shape(VZ, CX, BLK), shape(CX, BLK), shape(VZ * PB, BLK)),
        in_specs=[IN_VMEM] * 8 + [pl.BlockSpec(memory_space=pl.ANY)],
        out_specs=(IN_HBM, IN_VMEM, IN_VMEM),
        scratch_shapes=[pltpu.VMEM((VZ, CX, BLK), F32)] + choosing(1) + [
            pltpu.VMEM((2, VZ * PB, NOPS * BLK), BF16),
            pltpu.SemaphoreType.DMA((V,)),
        ],
        compiler_params=params,
    )(
        x_even, new, side_fix, fields, side, banks, radiative_mean_kelvin, parent_slab.reshape(VZ * PB, BLK), part_y,
    )
    parent_new = so_far + 0.5 * (got_y + got_x)
    return states.reshape(child_state.shape), parent_new.reshape(parent_slab.shape), comfort


def solution(mesh):
    placed = (
        P(None, None, "gx", "gy"),
        P(None, None, ("gx", "gy"), None),
        P(None, ("gx", "gy"), None),
        P("gx", "gy"),
        P(),
        P(),
        P(),
        P(None, "gx", "gy"),
        P(("gx", "gy"), None),
        P(("gx", "gy"), None),
        P(("gx", "gy"), None),
        P(),
        P("gx", "gy", None),
        P("gx", "gy", None),
        P("gx", "gy", None),
        P(),
    )
    return jax.shard_map(
        local,
        mesh=mesh,
        in_specs=placed,
        out_specs=(P(None, None, "gx", "gy"), P(None, None, ("gx", "gy"), None), P("gx", "gy")),
        check_vma=False,
    )
```

```python
import jax
import jax.numpy as jnp
from jax import lax
from jax.experimental import pallas as pl
from jax.experimental.pallas import tpu as pltpu
from jax.sharding import PartitionSpec as P

V, NZ, BLK, CX, K, KI, NOPS, PB = 4, 8, 128, 256, 16, 4, 8, 16
VZ = V * NZ
F32, BF16 = jnp.float32, jnp.bfloat16
PAD = 8
CHUNK = 64
EARLY = 3
VMEM_BYTES = 32 * 1024 * 1024

X_ROWS, X_PAR, X_IDX, X_ALL = 0, 64, 128, 144
Y_COLS, Y_PAR, Y_RELAY, Y_IDX, Y_RIDX, Y_ALL = 0, 128, 192, 256, 272, 288

IN_HBM = pl.BlockSpec(memory_space=pltpu.HBM)
IN_VMEM = pl.BlockSpec(memory_space=pltpu.VMEM)
IN_SMEM = pl.BlockSpec(memory_space=pltpu.SMEM)
NT = (((1,), (1,)), ((), ()))
TN = (((0,), (0,)), ((), ()))


def exchange(value, axis, odd):
    pairs = []
    for a in range(odd, lax.axis_size(axis) - 1, 2):
        pairs += [(a, a + 1), (a + 1, a)]
    return lax.ppermute(value, axis, pairs)


def one_lower(value, axis):
    return lax.ppermute(value, axis, [(a, a - 1) for a in range(1, lax.axis_size(axis))])


def split(value):
    high = value.astype(BF16)
    return high, (value - high.astype(F32)).astype(BF16)


def lanes(shape):
    return lax.broadcasted_iota(jnp.int32, shape, len(shape) - 1)


def rows_kernel(child, parent, tile, row, op, even, odd, first, last, blocks, names, stage, sems):
    copies = [
        pltpu.make_async_copy(child.at[:, pl.ds(0, 8)], first, sems.at[0]),
        pltpu.make_async_copy(child.at[:, pl.ds(CX - 8, 8)], last, sems.at[1]),
        pltpu.make_async_copy(parent, blocks, sems.at[2]),
    ] + [pltpu.make_async_copy(a, names.at[i], sems.at[3 + i]) for i, a in enumerate((tile, row, op))]
    for c in copies:
        c.start()
    stage[...] = jnp.zeros_like(stage)
    for c in copies:
        c.wait()
    for i in range(3):
        stage[i, :, 0:K] = names[i].astype(F32)
    index = stage[0] + pltpu.roll(stage[1], K, 1) + pltpu.roll(stage[2], 2 * K, 1)
    flag = lax.axis_index("gx") % 2 == 0
    for buffer in (even, odd):
        buffer[X_PAR:X_IDX] = blocks[...]
        buffer[X_IDX:X_ALL] = index
    for vz in range(VZ):
        low, high = first[vz, 0:2], last[vz, 6:8]
        even[2 * vz : 2 * vz + 2] = jnp.where(flag, high, low)
        odd[2 * vz : 2 * vz + 2] = jnp.where(flag, low, high)


def edges_kernel(courant_x, courant_y, diffusion, child, cells, to_next, to_prev, inner, sems):
    copies = [
        pltpu.make_async_copy(child.at[pl.ds(NZ * v, NZ)], cells.at[pl.ds(NZ * v, NZ), pl.ds(PAD, CX)], sems.at[v])
        for v in range(V)
    ]
    for c in copies:
        c.start()
    for vz in range(VZ):
        cells[vz, 0:PAD] = jnp.zeros((PAD, BLK), F32)
        cells[vz, PAD + CX : PAD + CX + PAD] = jnp.zeros((PAD, BLK), F32)
    which = lanes((CX, BLK)) // 4
    edges = jnp.zeros((CX, BLK), F32)
    for v in range(V):
        copies[v].wait()
        for z in range(NZ):
            vz = NZ * v + z
            edges = jnp.where(which == vz, pltpu.roll(cells[vz, PAD : PAD + CX], (4 * vz + 2) % BLK, 1), edges)
    half = CX // 2
    upper = lanes((half, BLK)) % 4 >= 2
    to_next[...] = jnp.where(upper, pltpu.roll(edges[half:], 2, 1), edges[:half])
    to_prev[...] = jnp.where(upper, edges[:half], pltpu.roll(edges[half:], BLK - 2, 1))
    step_inside(0, EARLY, courant_x, courant_y, diffusion, cells, inner)


def join_kernel(even_x, odd_x, own_even, to_next, to_prev, even, odd):
    flag_x, flag = lax.axis_index("gx") % 2 == 0, lax.axis_index("gy") % 2 == 0
    even[Y_COLS:Y_PAR] = jnp.where(flag, to_next[...], to_prev[...])
    odd[Y_COLS:Y_PAR] = jnp.where(flag, to_prev[...], to_next[...])
    relay = jnp.where(flag_x, odd_x[X_PAR:X_ALL], even_x[X_PAR:X_ALL])
    own = own_even[X_PAR:X_ALL]
    for buffer in (even, odd):
        buffer[Y_PAR:Y_RELAY] = own[:64]
        buffer[Y_RELAY:Y_IDX] = relay[:64]
        buffer[Y_IDX:Y_RIDX] = own[64:]
        buffer[Y_RIDX:Y_ALL] = relay[64:]


def coefficients(courant):
    size = jnp.abs(courant)
    half = 0.5 * size
    return half * size - 1.5 * size, 2.0 * size - size * size, half * size - half


def step_inside(first, last, courant_x, courant_y, diffusion, cells, inner):
    lane = lanes((8, BLK))[0:1]

    def variable(v, carry):
        d = diffusion[v]
        for z in range(NZ):
            sx, sy = courant_x[z], courant_y[z]
            own_x, near_x, far_x = coefficients(sx)
            own_y, near_y, far_y = coefficients(sy)
            up_x, up_y = sx >= 0.0, sy >= 0.0
            own = 1.0 + own_x + own_y - 6.0 * d
            low_x = d + jnp.where(up_x, near_x, 0.0)
            high_x = d + jnp.where(up_x, 0.0, near_x)
            low_far = jnp.where(up_x, far_x, 0.0)
            high_far = jnp.where(up_x, 0.0, far_x)
            low_y = jnp.where(lane == 0, 0.0, d + jnp.where(up_y, near_y, 0.0))
            high_y = jnp.where(lane == BLK - 1, 0.0, d + jnp.where(up_y, 0.0, near_y))
            outside = jnp.where(up_y, 0, BLK - 2)
            far = jnp.where((lane >= outside) & (lane < outside + 2), 0.0, far_y)
            turn_far = jnp.where(up_y, 2, BLK - 2)
            vz = NZ * v + z
            for r in range(PAD, PAD + CX, CHUNK):
                c = cells[vz, r : r + CHUNK]
                total = own * c
                total = total + low_x * cells[vz, r - 1 : r - 1 + CHUNK]
                total = total + high_x * cells[vz, r + 1 : r + 1 + CHUNK]
                total = total + low_far * cells[vz, r - 2 : r - 2 + CHUNK]
                total = total + high_far * cells[vz, r + 2 : r + 2 + CHUNK]
                total = total + low_y * pltpu.roll(c, 1, 1)
                total = total + high_y * pltpu.roll(c, BLK - 1, 1)
                total = total + far * pltpu.roll(c, turn_far, 1)
                beside = None
                if z < NZ - 1:
                    beside = cells[vz + 1, r : r + CHUNK]
                if z > 0:
                    below = cells[vz - 1, r : r + CHUNK]
                    beside = below if beside is None else beside + below
                inner[vz, r - PAD : r - PAD + CHUNK] = total + d * beside
        return carry

    lax.fori_loop(first, last, variable, 0)


def per_level(values, level):
    out = jnp.zeros(level.shape, F32)
    for z in range(NZ):
        out = jnp.where(level == z, values[z], out)
    return out


def choose(names, tile, select, at=0):
    rows = pltpu.roll(names, BLK - K, 1)
    ops = pltpu.roll(names, BLK - 2 * K, 1)
    codes = jnp.where(names == float(tile), ops * float(CX) + rows, -1.0)
    spread = [jnp.broadcast_to(codes[:, k : k + 1], (PB, CX)) for k in range(K)]
    cell = lanes((PB, CX)).astype(F32)
    for o in range(NOPS):
        total = jnp.zeros((PB, CX), F32)
        for k in range(K):
            total = total + jnp.where(spread[k] == cell + float(CX * o), 1.0, 0.0)
        total = total.astype(BF16)
        row = (select.shape[0] // NOPS) * o + PB * at
        select[row : row + PB, 0:CX] = total
        select[row : row + PB, CX : 2 * CX] = total


def turn_of(vz):
    return (2 * BLK - 2 - 4 * vz) % BLK


def at_edges(rows):
    return (lanes((rows, BLK)) + 2) % BLK < 4


def through_banks(picked, banks):
    both = lax.dot_general(picked[0], banks[...], NT, preferred_element_type=F32)
    rest = lax.dot_general(picked[1], banks[0:BLK], NT, preferred_element_type=F32)
    return both[:, :BLK] + both[:, BLK:] + rest


def gather_all(select, fields, side, edge, picked):
    rows = select.shape[0]
    many = rows // NOPS
    edge[...] = jnp.dot(select[...], side[...], preferred_element_type=F32)
    near = at_edges(rows)

    def one_pair(i, carry):
        pair = fields[:, pl.ds(pl.multiple_of(2 * BLK * i, 2 * BLK), 2 * BLK)]
        found = jnp.dot(select[...], pair, preferred_element_type=F32)
        for e in range(2):
            vz = 2 * i + e
            whole = found[:, BLK * e : BLK * (e + 1)] + jnp.where(near, pltpu.roll(edge[...], turn_of(vz), 1), 0.0)
            for part, value in enumerate(split(whole)):
                for o in range(NOPS):
                    picked[part, pl.ds(pl.multiple_of(many * vz, many), many), BLK * o : BLK * (o + 1)] = value[
                        many * o : many * (o + 1)
                    ]
        return carry

    lax.fori_loop(0, VZ // 2, one_pair, 0, unroll=True)


def ghost_part(blocks, coarse_banks, counts, table):
    high, low = split(jnp.concatenate([blocks[t][PB * v : PB * (v + 1)] for v in range(V) for t in range(2)], axis=0))
    for o in range(NOPS):
        bank_high, bank_low = (coarse_banks[i, BLK * o : BLK * (o + 1)] for i in range(2))
        made = (
            lax.dot_general(high, bank_high, NT, preferred_element_type=F32)
            + lax.dot_general(high, bank_low, NT, preferred_element_type=F32)
            + lax.dot_general(low, bank_high, NT, preferred_element_type=F32)
        )
        made_high, made_low = split(made)
        for v in range(V):
            table[32 * o : 32 * (o + 1), BLK * v : BLK * (v + 1)] = made_high[32 * v : 32 * (v + 1)]
            table[256 + 32 * o : 256 + 32 * (o + 1), BLK * v : BLK * (v + 1)] = made_low[32 * v : 32 * (v + 1)]
    return jnp.dot(counts, table[0:256], preferred_element_type=F32) + jnp.dot(
        counts, table[256:512], preferred_element_type=F32
    )


def middle_kernel(
    courant_x, courant_y, diffusion, so_far, cells, walls, fine, coarse, code, own_x, even_x, odd_x, after,
    inner, fields, banks, coarse_banks, counts_y, side_weights, open_sides, ghost, above_fix, below_fix, table,
):
    del so_far, after
    flag_x = lax.axis_index("gx") % 2 == 0
    prev_x = jnp.where(flag_x, odd_x[...], even_x[...])

    def weights(courant, level, variable):
        d = jnp.zeros(level.shape, F32)
        for v in range(V):
            d = jnp.where(variable == v, diffusion[v], d)
        s = per_level(courant, level)
        _, near, far = coefficients(s)
        up = s >= 0.0
        return (
            d + jnp.where(up, near, 0.0), d + jnp.where(up, 0.0, near), jnp.where(up, far, 0.0), jnp.where(up, 0.0, far),
        )

    next_rows = jnp.where(flag_x, even_x[X_ROWS:X_PAR], odd_x[X_ROWS:X_PAR])
    prev_rows = prev_x[X_ROWS:X_PAR]
    line = lax.broadcasted_iota(jnp.int32, (2 * VZ, BLK), 0)
    low, high, low_far, high_far = weights(courant_x, (line // 2) % NZ, line // (2 * NZ))
    first = line % 2 == 0
    above_fix[...] = low_far * prev_rows + jnp.where(first, low * pltpu.roll(prev_rows, 2 * VZ - 1, 0), 0.0)
    below_fix[...] = high_far * next_rows + jnp.where(first, 0.0, high * pltpu.roll(next_rows, 1, 0))

    lane = lanes((8, BLK))
    low, high, low_far, high_far = weights(courant_y, (lane // 4) % NZ, lane // (4 * NZ))
    place = lane % 4
    side_weights[0:8] = jnp.where(place < 2, high_far, 0.0)
    side_weights[8:16] = jnp.where(place == 1, high, 0.0)
    side_weights[16:24] = jnp.where(place == 2, low, 0.0)
    side_weights[24:32] = jnp.where(place >= 2, low_far, 0.0)
    for v in range(V):
        side_weights[32 + 8 * v : 40 + 8 * v] = jnp.full((8, BLK), diffusion[v], F32)

    for o in range(NOPS):
        high, low = split(fine[o])
        banks[0:BLK, BLK * o : BLK * (o + 1)] = high
        banks[BLK : 2 * BLK, BLK * o : BLK * (o + 1)] = low
        high, low = split(coarse[o])
        coarse_banks[0, BLK * o : BLK * (o + 1)] = high
        coarse_banks[1, BLK * o : BLK * (o + 1)] = low

    wanted = lax.broadcasted_iota(jnp.int32, (512, CX), 0)
    total = jnp.zeros((512, CX), F32)
    for k in range(KI):
        total = total + jnp.where(code[k : k + 1, :] == wanted, 1.0, 0.0)
    counts_y[...] = total[CX:].T.astype(BF16)
    made = ghost_part([own_x[X_PAR:X_IDX], prev_x[X_PAR:X_IDX]], coarse_banks, total[:CX].T.astype(BF16), table)
    for v in range(V):
        ghost[:, BLK * v : BLK * (v + 1)] = diffusion[v] * made[:, BLK * v : BLK * (v + 1)]
    step_inside(EARLY, V, courant_x, courant_y, diffusion, cells, inner)

    for r in range(0, CX, CHUNK):
        level = lanes((CHUNK, BLK)) // 4
        marks = jnp.zeros((CHUNK, BLK), F32)
        for z in range(NZ):
            wall = jnp.where(walls[z, r : r + CHUNK] == 1, 0.0, 1.0)
            marks = jnp.where(level == z, pltpu.roll(wall, 4 * z + 2, 1), marks)
        total = marks
        for v in range(1, V):
            total = total + pltpu.roll(marks, 4 * NZ * v, 1)
        open_sides[r : r + CHUNK] = total

    no_rows = jnp.zeros((6, BLK), F32)

    def variable(v, carry):
        for z in range(NZ):
            vz = NZ * v + z
            for r in range(0, CX, CHUNK):
                total = inner[vz, r : r + CHUNK]
                if z == NZ - 1:
                    total = total + ghost[r : r + CHUNK, pl.ds(pl.multiple_of(BLK * v, BLK), BLK)]
                if r == 0:
                    fix = jnp.concatenate([above_fix[pl.ds(2 * vz, 2)], no_rows], axis=0)
                    total = jnp.concatenate([total[:8] + fix, total[8:]], axis=0)
                if r == CX - CHUNK:
                    fix = jnp.concatenate([no_rows, below_fix[pl.ds(2 * vz, 2)]], axis=0)
                    total = jnp.concatenate([total[:-8], total[-8:] + fix], axis=0)
                total = jnp.where(walls[z, r : r + CHUNK] == 1, 0.0, total)
                inner[vz, r : r + CHUNK] = total
                high, low = split(total)
                columns = pl.ds(pl.multiple_of(BLK * vz, BLK), BLK)
                fields[r : r + CHUNK, columns] = high
                fields[CX + r : CX + r + CHUNK, columns] = low
        return carry

    lax.fori_loop(0, V, variable, 0)


def update_kernel(
    old, old_fields, walls, even_y, odd_y, banks, coarse_banks, counts_y, side_weights, open_sides,
    new, fields, side_fix, side, part_both,
    select, edge, table, picked,
):
    del old, old_fields
    flag_y = lax.axis_index("gy") % 2 == 0
    prev_y = jnp.where(flag_y, odd_y[...], even_y[...])

    half = CX // 2
    next_y = jnp.where(flag_y, even_y[Y_COLS:Y_PAR], odd_y[Y_COLS:Y_PAR])
    before = prev_y[Y_COLS:Y_PAR]
    upper = lanes((half, BLK)) % 4 >= 2
    by_minus_2, by_minus_1, by_plus_1, by_plus_2 = (side_weights[8 * i : 8 * i + 1] for i in range(4))
    for part in range(2):
        at = slice(half * part, half * (part + 1))
        if part == 0:
            columns = jnp.where(upper, next_y, before)
        else:
            columns = jnp.where(upper, pltpu.roll(next_y, 2, 1), pltpu.roll(before, BLK - 2, 1))
        total = (
            by_minus_2 * pltpu.roll(columns, BLK - 2, 1)
            + by_minus_1 * pltpu.roll(columns, BLK - 1, 1)
            + by_plus_1 * pltpu.roll(columns, 1, 1)
            + by_plus_2 * pltpu.roll(columns, 2, 1)
        )
        total = jnp.where(open_sides[at] > 0.5, total, 0.0)
        side_fix[at] = total
        side[at], side[CX + half * part : CX + half * (part + 1)] = split(total)

    made = ghost_part([prev_y[Y_PAR:Y_RELAY], prev_y[Y_RELAY:Y_IDX]], coarse_banks, counts_y[...], table)
    for v in range(V):
        vz = NZ * v + NZ - 1
        added = side_weights[32 + 8 * v : 33 + 8 * v] * made[:, BLK * v : BLK * (v + 1)]
        total = new[vz] + jnp.where(walls[NZ - 1] == 1, 0.0, added)
        new[vz] = total
        columns = slice(BLK * vz, BLK * (vz + 1))
        fields[0:CX, columns], fields[CX : 2 * CX, columns] = split(total)

    choose(prev_y[Y_RIDX:Y_ALL], 3, select)
    gather_all(select, fields, side, edge, picked)
    part_both[...] = through_banks(picked, banks)


def sides_kernel(even_x, odd_x, even_y, odd_y, fields, side, banks, part_x, part_y, select, edge, picked):
    flag_x, flag_y = lax.axis_index("gx") % 2 == 0, lax.axis_index("gy") % 2 == 0
    choose(jnp.where(flag_x, odd_x[X_IDX:X_ALL], even_x[X_IDX:X_ALL]), 1, select, 0)
    choose(jnp.where(flag_y, odd_y[Y_IDX:Y_RIDX], even_y[Y_IDX:Y_RIDX]), 2, select, 1)
    gather_all(select, fields, side, edge, picked)
    result = through_banks(picked, banks)
    for vz in range(VZ):
        part_x[PB * vz : PB * (vz + 1)] = result[2 * PB * vz : 2 * PB * vz + PB]
        part_y[PB * vz : PB * (vz + 1)] = result[2 * PB * vz + PB : 2 * PB * (vz + 1)]


def add_kernel(part_x, got_both, part_y, to_x, to_y):
    to_x[...] = part_x[...] + got_both[...]
    to_y[...] = part_y[...]


def own_kernel(
    own_x, new, side_fix, fields, side, banks, radiant, slab, after,
    states, comfort, so_far,
    whole, select, edge, picked, sems,
):
    del after
    near = at_edges(CHUNK)

    def variable(v, carry):
        for z in range(NZ):
            vz = NZ * v + z
            for r in range(0, CX, CHUNK):
                turned = pltpu.roll(side_fix[r : r + CHUNK], turn_of(vz), 1)
                whole[vz, r : r + CHUNK] = new[vz, r : r + CHUNK] + jnp.where(near, turned, 0.0)
        pltpu.make_async_copy(whole.at[pl.ds(NZ * v, NZ)], states.at[pl.ds(NZ * v, NZ)], sems.at[v]).start()
        return carry

    lax.fori_loop(0, V, variable, 0)
    u, w, t, h = (whole[NZ * v] for v in range(V))
    speed = jnp.sqrt(u * u + w * w + 0.25)
    excess = radiant[...] - t
    comfort[...] = t + 0.3 * excess - 0.6 * (speed - 1.0) + 0.4 * h + 0.1 * t * excess - 0.15 * speed * excess
    choose(own_x[X_IDX:X_ALL], 0, select)
    gather_all(select, fields, side, edge, picked)
    so_far[...] = 0.5 * slab[...] + 0.5 * through_banks(picked, banks)
    for v in range(V):
        pltpu.make_async_copy(whole.at[pl.ds(NZ * v, NZ)], states.at[pl.ds(NZ * v, NZ)], sems.at[v]).wait()


def shape(*dims, kind=F32):
    return jax.ShapeDtypeStruct(dims, kind)


def local(
    child_state, parent_slab, parent_above, radiative_mean_kelvin, courant_x, courant_y, diffusion, building,
    fine_tile, fine_row, fine_op, fine_bank, coarse_tile, coarse_row, coarse_op, coarse_bank,
):
    child = child_state.reshape(VZ, CX, BLK)
    parent = parent_above.reshape(V * PB, BLK)
    params = pltpu.CompilerParams(vmem_limit_bytes=VMEM_BYTES)
    x_even, x_odd = pl.pallas_call(
        rows_kernel,
        out_shape=(shape(X_ALL, BLK), shape(X_ALL, BLK)),
        in_specs=[IN_HBM] * 5,
        out_specs=(IN_VMEM,) * 2,
        scratch_shapes=[
            pltpu.VMEM((VZ, 8, BLK), F32), pltpu.VMEM((VZ, 8, BLK), F32), pltpu.VMEM((V * PB, BLK), F32),
            pltpu.VMEM((3, PB, K), jnp.int32), pltpu.VMEM((3, PB, BLK), F32), pltpu.SemaphoreType.DMA((6,)),
        ],
        compiler_params=params,
    )(*(pltpu.with_memory_space_constraint(a, pltpu.HBM) for a in (child, parent, fine_tile, fine_row, fine_op)))
    got_x_even = exchange(x_even, "gx", 0)
    got_x_odd = exchange(x_odd, "gx", 1)
    coarse_code = ((coarse_tile >> 1) * 256 + coarse_op * 32 + (coarse_tile & 1) * PB + coarse_row).reshape(CX, KI).T
    cells, to_next, to_prev, inner = pl.pallas_call(
        edges_kernel,
        out_shape=(
            shape(VZ, CX + 2 * PAD, BLK), shape(CX // 2, BLK), shape(CX // 2, BLK), shape(VZ, CX, BLK),
        ),
        in_specs=[IN_SMEM] * 3 + [IN_HBM],
        out_specs=(IN_VMEM,) * 4,
        scratch_shapes=[pltpu.SemaphoreType.DMA((V,))],
        compiler_params=params,
    )(courant_x, courant_y, diffusion, child)
    y_even, y_odd = pl.pallas_call(
        join_kernel,
        out_shape=(shape(Y_ALL, BLK), shape(Y_ALL, BLK)),
        in_specs=[IN_VMEM] * 5,
        out_specs=(IN_VMEM,) * 2,
        compiler_params=params,
    )(got_x_even, got_x_odd, x_even, to_next, to_prev)
    got_y_odd = exchange(y_odd, "gy", 1)
    got_y_even = exchange(y_even, "gy", 0)
    fields_shape = shape(2 * CX, VZ * BLK, kind=BF16)
    inner, fields, banks, coarse_banks, counts_y, side_weights, open_sides = pl.pallas_call(
        middle_kernel,
        out_shape=(
            shape(VZ, CX, BLK), fields_shape, shape(2 * BLK, NOPS * BLK, kind=BF16), shape(2, NOPS * BLK, BLK, kind=BF16),
            shape(CX, CX, kind=BF16), shape(64, BLK), shape(CX, BLK),
        ),
        in_specs=[IN_SMEM] * 3 + [IN_VMEM] * 9 + [pl.BlockSpec(memory_space=pl.ANY)],
        out_specs=(IN_VMEM,) * 7,
        input_output_aliases={3: 0},
        scratch_shapes=[
            pltpu.VMEM((CX, V * BLK), F32),
            pltpu.VMEM((2 * VZ, BLK), F32),
            pltpu.VMEM((2 * VZ, BLK), F32),
            pltpu.VMEM((512, V * BLK), BF16),
        ],
        compiler_params=params,
    )(
        courant_x, courant_y, diffusion, inner, cells, building, fine_bank, coarse_bank, coarse_code,
        x_even, got_x_even, got_x_odd, y_even,
    )

    def choosing(tiles):
        rows = tiles * NOPS * PB
        return [
            pltpu.VMEM((rows, 2 * CX), BF16),
            pltpu.VMEM((rows, BLK), F32),
        ]

    new, fields, side_fix, side, part_both = pl.pallas_call(
        update_kernel,
        out_shape=(
            shape(VZ, CX, BLK), fields_shape, shape(CX, BLK), shape(2 * CX, BLK, kind=BF16), shape(VZ * PB, BLK),
        ),
        in_specs=[IN_VMEM] * 10,
        out_specs=(IN_VMEM,) * 5,
        input_output_aliases={0: 0, 1: 1},
        scratch_shapes=choosing(1) + [
            pltpu.VMEM((512, V * BLK), BF16),
            pltpu.VMEM((2, VZ * PB, NOPS * BLK), BF16),
        ],
        compiler_params=params,
    )(inner, fields, building, got_y_even, got_y_odd, banks, coarse_banks, counts_y, side_weights, open_sides)
    got_both = one_lower(part_both, "gy")
    part_x, part_y = pl.pallas_call(
        sides_kernel,
        out_shape=(shape(VZ * PB, BLK),) * 2,
        in_specs=[IN_VMEM] * 7,
        out_specs=(IN_VMEM,) * 2,
        scratch_shapes=choosing(2) + [pltpu.VMEM((2, 2 * VZ * PB, NOPS * BLK), BF16)],
        compiler_params=params,
    )(got_x_even, got_x_odd, got_y_even, got_y_odd, fields, side, banks)
    got_x = one_lower(part_x + got_both, "gx")
    got_y = one_lower(part_y, "gy")
    states, comfort, so_far = pl.pallas_call(
        own_kernel,
        out_shape=(shape(VZ, CX, BLK), shape(CX, BLK), shape(VZ * PB, BLK)),
        in_specs=[IN_VMEM] * 8 + [pl.BlockSpec(memory_space=pl.ANY)],
        out_specs=(IN_HBM, IN_VMEM, IN_VMEM),
        scratch_shapes=[pltpu.VMEM((VZ, CX, BLK), F32)] + choosing(1) + [
            pltpu.VMEM((2, VZ * PB, NOPS * BLK), BF16),
            pltpu.SemaphoreType.DMA((V,)),
        ],
        compiler_params=params,
    )(
        x_even, new, side_fix, fields, side, banks, radiative_mean_kelvin, parent_slab.reshape(VZ * PB, BLK), part_y,
    )
    parent_new = so_far + 0.5 * (got_y + got_x)
    return states.reshape(child_state.shape), parent_new.reshape(parent_slab.shape), comfort


def solution(mesh):
    placed = (
        P(None, None, "gx", "gy"),
        P(None, None, ("gx", "gy"), None),
        P(None, ("gx", "gy"), None),
        P("gx", "gy"),
        P(),
        P(),
        P(),
        P(None, "gx", "gy"),
        P(("gx", "gy"), None),
        P(("gx", "gy"), None),
        P(("gx", "gy"), None),
        P(),
        P("gx", "gy", None),
        P("gx", "gy", None),
        P("gx", "gy", None),
        P(),
    )
    return jax.shard_map(
        local,
        mesh=mesh,
        in_specs=placed,
        out_specs=(P(None, None, "gx", "gy"), P(None, None, ("gx", "gy"), None), P("gx", "gy")),
        check_vma=False,
    )
```

```python
import jax
import jax.numpy as jnp
from jax import lax
from jax.experimental import pallas as pl
from jax.experimental.pallas import tpu as pltpu
from jax.sharding import PartitionSpec as P

V, NZ, BLK, CX, K, KI, NOPS, PB = 4, 8, 128, 256, 16, 4, 8, 16
VZ = V * NZ
F32, BF16 = jnp.float32, jnp.bfloat16
PAD = 8
CHUNK = 64
EARLY = 3
VMEM_BYTES = 32 * 1024 * 1024

X_ROWS, X_PAR, X_IDX, X_ALL = 0, 64, 128, 144
Y_COLS, Y_PAR, Y_RELAY, Y_IDX, Y_RIDX, Y_ALL = 0, 128, 192, 256, 272, 288

IN_HBM = pl.BlockSpec(memory_space=pltpu.HBM)
IN_VMEM = pl.BlockSpec(memory_space=pltpu.VMEM)
IN_SMEM = pl.BlockSpec(memory_space=pltpu.SMEM)
NT = (((1,), (1,)), ((), ()))
TN = (((0,), (0,)), ((), ()))


def exchange(value, axis, odd):
    pairs = []
    for a in range(odd, lax.axis_size(axis) - 1, 2):
        pairs += [(a, a + 1), (a + 1, a)]
    return lax.ppermute(value, axis, pairs)


def one_lower(value, axis):
    return lax.ppermute(value, axis, [(a, a - 1) for a in range(1, lax.axis_size(axis))])


def split(value):
    high = value.astype(BF16)
    return high, (value - high.astype(F32)).astype(BF16)


def lanes(shape):
    return lax.broadcasted_iota(jnp.int32, shape, len(shape) - 1)


def rows_kernel(child, parent, tile, row, op, even, odd, first, last, blocks, names, stage, sems):
    copies = [
        pltpu.make_async_copy(child.at[:, pl.ds(0, 8)], first, sems.at[0]),
        pltpu.make_async_copy(child.at[:, pl.ds(CX - 8, 8)], last, sems.at[1]),
        pltpu.make_async_copy(parent, blocks, sems.at[2]),
    ] + [pltpu.make_async_copy(a, names.at[i], sems.at[3 + i]) for i, a in enumerate((tile, row, op))]
    for c in copies:
        c.start()
    stage[...] = jnp.zeros_like(stage)
    for c in copies:
        c.wait()
    for i in range(3):
        stage[i, :, 0:K] = names[i].astype(F32)
    index = stage[0] + pltpu.roll(stage[1], K, 1) + pltpu.roll(stage[2], 2 * K, 1)
    flag = lax.axis_index("gx") % 2 == 0
    for buffer in (even, odd):
        buffer[X_PAR:X_IDX] = blocks[...]
        buffer[X_IDX:X_ALL] = index
    for vz in range(VZ):
        low, high = first[vz, 0:2], last[vz, 6:8]
        even[2 * vz : 2 * vz + 2] = jnp.where(flag, high, low)
        odd[2 * vz : 2 * vz + 2] = jnp.where(flag, low, high)


def edges_kernel(courant_x, courant_y, diffusion, child, cells, to_next, to_prev, inner, sems):
    copies = [
        pltpu.make_async_copy(child.at[pl.ds(NZ * v, NZ)], cells.at[pl.ds(NZ * v, NZ), pl.ds(PAD, CX)], sems.at[v])
        for v in range(V)
    ]
    for c in copies:
        c.start()
    for vz in range(VZ):
        cells[vz, 0:PAD] = jnp.zeros((PAD, BLK), F32)
        cells[vz, PAD + CX : PAD + CX + PAD] = jnp.zeros((PAD, BLK), F32)
    which = lanes((CX, BLK)) // 4
    edges = jnp.zeros((CX, BLK), F32)
    for v in range(V):
        copies[v].wait()
        for z in range(NZ):
            vz = NZ * v + z
            edges = jnp.where(which == vz, pltpu.roll(cells[vz, PAD : PAD + CX], (4 * vz + 2) % BLK, 1), edges)
    half = CX // 2
    upper = lanes((half, BLK)) % 4 >= 2
    to_next[...] = jnp.where(upper, pltpu.roll(edges[half:], 2, 1), edges[:half])
    to_prev[...] = jnp.where(upper, edges[:half], pltpu.roll(edges[half:], BLK - 2, 1))
    step_inside(0, EARLY, courant_x, courant_y, diffusion, cells, inner)


def join_kernel(even_x, odd_x, own_even, to_next, to_prev, even, odd):
    flag_x, flag = lax.axis_index("gx") % 2 == 0, lax.axis_index("gy") % 2 == 0
    even[Y_COLS:Y_PAR] = jnp.where(flag, to_next[...], to_prev[...])
    odd[Y_COLS:Y_PAR] = jnp.where(flag, to_prev[...], to_next[...])
    relay = jnp.where(flag_x, odd_x[X_PAR:X_ALL], even_x[X_PAR:X_ALL])
    own = own_even[X_PAR:X_ALL]
    for buffer in (even, odd):
        buffer[Y_PAR:Y_RELAY] = own[:64]
        buffer[Y_RELAY:Y_IDX] = relay[:64]
        buffer[Y_IDX:Y_RIDX] = own[64:]
        buffer[Y_RIDX:Y_ALL] = relay[64:]


def coefficients(courant):
    size = jnp.abs(courant)
    half = 0.5 * size
    return half * size - 1.5 * size, 2.0 * size - size * size, half * size - half


def step_inside(first, last, courant_x, courant_y, diffusion, cells, inner):
    lane = lanes((8, BLK))[0:1]

    def variable(v, carry):
        d = diffusion[v]
        for z in range(NZ):
            sx, sy = courant_x[z], courant_y[z]
            own_x, near_x, far_x = coefficients(sx)
            own_y, near_y, far_y = coefficients(sy)
            up_x, up_y = sx >= 0.0, sy >= 0.0
            own = 1.0 + own_x + own_y - 6.0 * d
            low_x = d + jnp.where(up_x, near_x, 0.0)
            high_x = d + jnp.where(up_x, 0.0, near_x)
            low_far = jnp.where(up_x, far_x, 0.0)
            high_far = jnp.where(up_x, 0.0, far_x)
            low_y = jnp.where(lane == 0, 0.0, d + jnp.where(up_y, near_y, 0.0))
            high_y = jnp.where(lane == BLK - 1, 0.0, d + jnp.where(up_y, 0.0, near_y))
            outside = jnp.where(up_y, 0, BLK - 2)
            far = jnp.where((lane >= outside) & (lane < outside + 2), 0.0, far_y)
            turn_far = jnp.where(up_y, 2, BLK - 2)
            vz = NZ * v + z
            for r in range(PAD, PAD + CX, CHUNK):
                c = cells[vz, r : r + CHUNK]
                total = own * c
                total = total + low_x * cells[vz, r - 1 : r - 1 + CHUNK]
                total = total + high_x * cells[vz, r + 1 : r + 1 + CHUNK]
                total = total + low_far * cells[vz, r - 2 : r - 2 + CHUNK]
                total = total + high_far * cells[vz, r + 2 : r + 2 + CHUNK]
                total = total + low_y * pltpu.roll(c, 1, 1)
                total = total + high_y * pltpu.roll(c, BLK - 1, 1)
                total = total + far * pltpu.roll(c, turn_far, 1)
                beside = None
                if z < NZ - 1:
                    beside = cells[vz + 1, r : r + CHUNK]
                if z > 0:
                    below = cells[vz - 1, r : r + CHUNK]
                    beside = below if beside is None else beside + below
                inner[vz, r - PAD : r - PAD + CHUNK] = total + d * beside
        return carry

    lax.fori_loop(first, last, variable, 0, unroll=last - first)


def per_level(values, level):
    out = jnp.zeros(level.shape, F32)
    for z in range(NZ):
        out = jnp.where(level == z, values[z], out)
    return out


def choose(names, tile, select, at=0):
    rows = pltpu.roll(names, BLK - K, 1)
    ops = pltpu.roll(names, BLK - 2 * K, 1)
    codes = jnp.where(names == float(tile), ops * float(CX) + rows, -1.0)
    spread = [jnp.broadcast_to(codes[:, k : k + 1], (PB, CX)) for k in range(K)]
    cell = lanes((PB, CX)).astype(F32)
    for o in range(NOPS):
        total = jnp.zeros((PB, CX), F32)
        for k in range(K):
            total = total + jnp.where(spread[k] == cell + float(CX * o), 1.0, 0.0)
        total = total.astype(BF16)
        row = (select.shape[0] // NOPS) * o + PB * at
        select[row : row + PB, 0:CX] = total
        select[row : row + PB, CX : 2 * CX] = total


def turn_of(vz):
    return (2 * BLK - 2 - 4 * vz) % BLK


def at_edges(rows):
    return (lanes((rows, BLK)) + 2) % BLK < 4


def through_banks(picked, banks):
    both = lax.dot_general(picked[0], banks[...], NT, preferred_element_type=F32)
    rest = lax.dot_general(picked[1], banks[0:BLK], NT, preferred_element_type=F32)
    return both[:, :BLK] + both[:, BLK:] + rest


def gather_all(select, fields, side, edge, picked):
    rows = select.shape[0]
    many = rows // NOPS
    edge[...] = jnp.dot(select[...], side[...], preferred_element_type=F32)
    near = at_edges(rows)

    def one_pair(i, carry):
        pair = fields[:, pl.ds(pl.multiple_of(2 * BLK * i, 2 * BLK), 2 * BLK)]
        found = jnp.dot(select[...], pair, preferred_element_type=F32)
        for e in range(2):
            vz = 2 * i + e
            whole = found[:, BLK * e : BLK * (e + 1)] + jnp.where(near, pltpu.roll(edge[...], turn_of(vz), 1), 0.0)
            for part, value in enumerate(split(whole)):
                for o in range(NOPS):
                    picked[part, pl.ds(pl.multiple_of(many * vz, many), many), BLK * o : BLK * (o + 1)] = value[
                        many * o : many * (o + 1)
                    ]
        return carry

    lax.fori_loop(0, VZ // 2, one_pair, 0, unroll=True)


def ghost_part(blocks, coarse_banks, counts, table):
    high, low = split(jnp.concatenate([blocks[t][PB * v : PB * (v + 1)] for v in range(V) for t in range(2)], axis=0))
    for o in range(NOPS):
        bank_high, bank_low = (coarse_banks[i, BLK * o : BLK * (o + 1)] for i in range(2))
        made = (
            lax.dot_general(high, bank_high, NT, preferred_element_type=F32)
            + lax.dot_general(high, bank_low, NT, preferred_element_type=F32)
            + lax.dot_general(low, bank_high, NT, preferred_element_type=F32)
        )
        made_high, made_low = split(made)
        for v in range(V):
            table[32 * o : 32 * (o + 1), BLK * v : BLK * (v + 1)] = made_high[32 * v : 32 * (v + 1)]
            table[256 + 32 * o : 256 + 32 * (o + 1), BLK * v : BLK * (v + 1)] = made_low[32 * v : 32 * (v + 1)]
    return jnp.dot(counts, table[0:256], preferred_element_type=F32) + jnp.dot(
        counts, table[256:512], preferred_element_type=F32
    )


def middle_kernel(
    courant_x, courant_y, diffusion, so_far, cells, walls, fine, coarse, code, own_x, even_x, odd_x, after,
    inner, fields, banks, coarse_banks, counts_y, side_weights, open_sides, ghost, above_fix, below_fix, table,
):
    del so_far, after
    flag_x = lax.axis_index("gx") % 2 == 0
    prev_x = jnp.where(flag_x, odd_x[...], even_x[...])

    def weights(courant, level, variable):
        d = jnp.zeros(level.shape, F32)
        for v in range(V):
            d = jnp.where(variable == v, diffusion[v], d)
        s = per_level(courant, level)
        _, near, far = coefficients(s)
        up = s >= 0.0
        return (
            d + jnp.where(up, near, 0.0), d + jnp.where(up, 0.0, near), jnp.where(up, far, 0.0), jnp.where(up, 0.0, far),
        )

    next_rows = jnp.where(flag_x, even_x[X_ROWS:X_PAR], odd_x[X_ROWS:X_PAR])
    prev_rows = prev_x[X_ROWS:X_PAR]
    line = lax.broadcasted_iota(jnp.int32, (2 * VZ, BLK), 0)
    low, high, low_far, high_far = weights(courant_x, (line // 2) % NZ, line // (2 * NZ))
    first = line % 2 == 0
    above_fix[...] = low_far * prev_rows + jnp.where(first, low * pltpu.roll(prev_rows, 2 * VZ - 1, 0), 0.0)
    below_fix[...] = high_far * next_rows + jnp.where(first, 0.0, high * pltpu.roll(next_rows, 1, 0))

    lane = lanes((8, BLK))
    low, high, low_far, high_far = weights(courant_y, (lane // 4) % NZ, lane // (4 * NZ))
    place = lane % 4
    side_weights[0:8] = jnp.where(place < 2, high_far, 0.0)
    side_weights[8:16] = jnp.where(place == 1, high, 0.0)
    side_weights[16:24] = jnp.where(place == 2, low, 0.0)
    side_weights[24:32] = jnp.where(place >= 2, low_far, 0.0)
    for v in range(V):
        side_weights[32 + 8 * v : 40 + 8 * v] = jnp.full((8, BLK), diffusion[v], F32)

    for o in range(NOPS):
        high, low = split(fine[o])
        banks[0:BLK, BLK * o : BLK * (o + 1)] = high
        banks[BLK : 2 * BLK, BLK * o : BLK * (o + 1)] = low
        high, low = split(coarse[o])
        coarse_banks[0, BLK * o : BLK * (o + 1)] = high
        coarse_banks[1, BLK * o : BLK * (o + 1)] = low

    wanted = lax.broadcasted_iota(jnp.int32, (512, CX), 0)
    total = jnp.zeros((512, CX), F32)
    for k in range(KI):
        total = total + jnp.where(code[k : k + 1, :] == wanted, 1.0, 0.0)
    counts_y[...] = total[CX:].T.astype(BF16)
    made = ghost_part([own_x[X_PAR:X_IDX], prev_x[X_PAR:X_IDX]], coarse_banks, total[:CX].T.astype(BF16), table)
    for v in range(V):
        ghost[:, BLK * v : BLK * (v + 1)] = diffusion[v] * made[:, BLK * v : BLK * (v + 1)]
    step_inside(EARLY, V, courant_x, courant_y, diffusion, cells, inner)

    for r in range(0, CX, CHUNK):
        level = lanes((CHUNK, BLK)) // 4
        marks = jnp.zeros((CHUNK, BLK), F32)
        for z in range(NZ):
            wall = jnp.where(walls[z, r : r + CHUNK] == 1, 0.0, 1.0)
            marks = jnp.where(level == z, pltpu.roll(wall, 4 * z + 2, 1), marks)
        total = marks
        for v in range(1, V):
            total = total + pltpu.roll(marks, 4 * NZ * v, 1)
        open_sides[r : r + CHUNK] = total

    no_rows = jnp.zeros((6, BLK), F32)

    def variable(v, carry):
        for z in range(NZ):
            vz = NZ * v + z
            for r in range(0, CX, CHUNK):
                total = inner[vz, r : r + CHUNK]
                if z == NZ - 1:
                    total = total + ghost[r : r + CHUNK, pl.ds(pl.multiple_of(BLK * v, BLK), BLK)]
                if r == 0:
                    fix = jnp.concatenate([above_fix[pl.ds(2 * vz, 2)], no_rows], axis=0)
                    total = jnp.concatenate([total[:8] + fix, total[8:]], axis=0)
                if r == CX - CHUNK:
                    fix = jnp.concatenate([no_rows, below_fix[pl.ds(2 * vz, 2)]], axis=0)
                    total = jnp.concatenate([total[:-8], total[-8:] + fix], axis=0)
                total = jnp.where(walls[z, r : r + CHUNK] == 1, 0.0, total)
                inner[vz, r : r + CHUNK] = total
                high, low = split(total)
                columns = pl.ds(pl.multiple_of(BLK * vz, BLK), BLK)
                fields[r : r + CHUNK, columns] = high
                fields[CX + r : CX + r + CHUNK, columns] = low
        return carry

    lax.fori_loop(0, V, variable, 0, unroll=2)


def update_kernel(
    old, old_fields, walls, even_y, odd_y, banks, coarse_banks, counts_y, side_weights, open_sides,
    new, fields, side_fix, side, part_both,
    select, edge, table, picked,
):
    del old, old_fields
    flag_y = lax.axis_index("gy") % 2 == 0
    prev_y = jnp.where(flag_y, odd_y[...], even_y[...])

    half = CX // 2
    next_y = jnp.where(flag_y, even_y[Y_COLS:Y_PAR], odd_y[Y_COLS:Y_PAR])
    before = prev_y[Y_COLS:Y_PAR]
    upper = lanes((half, BLK)) % 4 >= 2
    by_minus_2, by_minus_1, by_plus_1, by_plus_2 = (side_weights[8 * i : 8 * i + 1] for i in range(4))
    for part in range(2):
        at = slice(half * part, half * (part + 1))
        if part == 0:
            columns = jnp.where(upper, next_y, before)
        else:
            columns = jnp.where(upper, pltpu.roll(next_y, 2, 1), pltpu.roll(before, BLK - 2, 1))
        total = (
            by_minus_2 * pltpu.roll(columns, BLK - 2, 1)
            + by_minus_1 * pltpu.roll(columns, BLK - 1, 1)
            + by_plus_1 * pltpu.roll(columns, 1, 1)
            + by_plus_2 * pltpu.roll(columns, 2, 1)
        )
        total = jnp.where(open_sides[at] > 0.5, total, 0.0)
        side_fix[at] = total
        side[at], side[CX + half * part : CX + half * (part + 1)] = split(total)

    made = ghost_part([prev_y[Y_PAR:Y_RELAY], prev_y[Y_RELAY:Y_IDX]], coarse_banks, counts_y[...], table)
    for v in range(V):
        vz = NZ * v + NZ - 1
        added = side_weights[32 + 8 * v : 33 + 8 * v] * made[:, BLK * v : BLK * (v + 1)]
        total = new[vz] + jnp.where(walls[NZ - 1] == 1, 0.0, added)
        new[vz] = total
        columns = slice(BLK * vz, BLK * (vz + 1))
        fields[0:CX, columns], fields[CX : 2 * CX, columns] = split(total)

    choose(prev_y[Y_RIDX:Y_ALL], 3, select)
    gather_all(select, fields, side, edge, picked)
    part_both[...] = through_banks(picked, banks)


def sides_kernel(even_x, odd_x, even_y, odd_y, fields, side, banks, part_x, part_y, select, edge, picked):
    flag_x, flag_y = lax.axis_index("gx") % 2 == 0, lax.axis_index("gy") % 2 == 0
    choose(jnp.where(flag_x, odd_x[X_IDX:X_ALL], even_x[X_IDX:X_ALL]), 1, select, 0)
    choose(jnp.where(flag_y, odd_y[Y_IDX:Y_RIDX], even_y[Y_IDX:Y_RIDX]), 2, select, 1)
    gather_all(select, fields, side, edge, picked)
    result = through_banks(picked, banks)
    for vz in range(VZ):
        part_x[PB * vz : PB * (vz + 1)] = result[2 * PB * vz : 2 * PB * vz + PB]
        part_y[PB * vz : PB * (vz + 1)] = result[2 * PB * vz + PB : 2 * PB * (vz + 1)]


def add_kernel(part_x, got_both, part_y, to_x, to_y):
    to_x[...] = part_x[...] + got_both[...]
    to_y[...] = part_y[...]


def own_kernel(
    own_x, new, side_fix, fields, side, banks, radiant, slab, after,
    states, comfort, so_far,
    whole, select, edge, picked, sems,
):
    del after
    near = at_edges(CHUNK)

    def variable(v, carry):
        for z in range(NZ):
            vz = NZ * v + z
            for r in range(0, CX, CHUNK):
                turned = pltpu.roll(side_fix[r : r + CHUNK], turn_of(vz), 1)
                whole[vz, r : r + CHUNK] = new[vz, r : r + CHUNK] + jnp.where(near, turned, 0.0)
        pltpu.make_async_copy(whole.at[pl.ds(NZ * v, NZ)], states.at[pl.ds(NZ * v, NZ)], sems.at[v]).start()
        return carry

    lax.fori_loop(0, V, variable, 0, unroll=2)
    u, w, t, h = (whole[NZ * v] for v in range(V))
    speed = jnp.sqrt(u * u + w * w + 0.25)
    excess = radiant[...] - t
    comfort[...] = t + 0.3 * excess - 0.6 * (speed - 1.0) + 0.4 * h + 0.1 * t * excess - 0.15 * speed * excess
    choose(own_x[X_IDX:X_ALL], 0, select)
    gather_all(select, fields, side, edge, picked)
    so_far[...] = 0.5 * slab[...] + 0.5 * through_banks(picked, banks)
    for v in range(V):
        pltpu.make_async_copy(whole.at[pl.ds(NZ * v, NZ)], states.at[pl.ds(NZ * v, NZ)], sems.at[v]).wait()


def shape(*dims, kind=F32):
    return jax.ShapeDtypeStruct(dims, kind)


def local(
    child_state, parent_slab, parent_above, radiative_mean_kelvin, courant_x, courant_y, diffusion, building,
    fine_tile, fine_row, fine_op, fine_bank, coarse_tile, coarse_row, coarse_op, coarse_bank,
):
    child = child_state.reshape(VZ, CX, BLK)
    parent = parent_above.reshape(V * PB, BLK)
    params = pltpu.CompilerParams(vmem_limit_bytes=VMEM_BYTES)
    x_even, x_odd = pl.pallas_call(
        rows_kernel,
        out_shape=(shape(X_ALL, BLK), shape(X_ALL, BLK)),
        in_specs=[IN_HBM] * 5,
        out_specs=(IN_VMEM,) * 2,
        scratch_shapes=[
            pltpu.VMEM((VZ, 8, BLK), F32), pltpu.VMEM((VZ, 8, BLK), F32), pltpu.VMEM((V * PB, BLK), F32),
            pltpu.VMEM((3, PB, K), jnp.int32), pltpu.VMEM((3, PB, BLK), F32), pltpu.SemaphoreType.DMA((6,)),
        ],
        compiler_params=params,
    )(*(pltpu.with_memory_space_constraint(a, pltpu.HBM) for a in (child, parent, fine_tile, fine_row, fine_op)))
    got_x_even = exchange(x_even, "gx", 0)
    got_x_odd = exchange(x_odd, "gx", 1)
    coarse_code = ((coarse_tile >> 1) * 256 + coarse_op * 32 + (coarse_tile & 1) * PB + coarse_row).reshape(CX, KI).T
    cells, to_next, to_prev, inner = pl.pallas_call(
        edges_kernel,
        out_shape=(
            shape(VZ, CX + 2 * PAD, BLK), shape(CX // 2, BLK), shape(CX // 2, BLK), shape(VZ, CX, BLK),
        ),
        in_specs=[IN_SMEM] * 3 + [IN_HBM],
        out_specs=(IN_VMEM,) * 4,
        scratch_shapes=[pltpu.SemaphoreType.DMA((V,))],
        compiler_params=params,
    )(courant_x, courant_y, diffusion, child)
    y_even, y_odd = pl.pallas_call(
        join_kernel,
        out_shape=(shape(Y_ALL, BLK), shape(Y_ALL, BLK)),
        in_specs=[IN_VMEM] * 5,
        out_specs=(IN_VMEM,) * 2,
        compiler_params=params,
    )(got_x_even, got_x_odd, x_even, to_next, to_prev)
    got_y_odd = exchange(y_odd, "gy", 1)
    got_y_even = exchange(y_even, "gy", 0)
    fields_shape = shape(2 * CX, VZ * BLK, kind=BF16)
    inner, fields, banks, coarse_banks, counts_y, side_weights, open_sides = pl.pallas_call(
        middle_kernel,
        out_shape=(
            shape(VZ, CX, BLK), fields_shape, shape(2 * BLK, NOPS * BLK, kind=BF16), shape(2, NOPS * BLK, BLK, kind=BF16),
            shape(CX, CX, kind=BF16), shape(64, BLK), shape(CX, BLK),
        ),
        in_specs=[IN_SMEM] * 3 + [IN_VMEM] * 9 + [pl.BlockSpec(memory_space=pl.ANY)],
        out_specs=(IN_VMEM,) * 7,
        input_output_aliases={3: 0},
        scratch_shapes=[
            pltpu.VMEM((CX, V * BLK), F32),
            pltpu.VMEM((2 * VZ, BLK), F32),
            pltpu.VMEM((2 * VZ, BLK), F32),
            pltpu.VMEM((512, V * BLK), BF16),
        ],
        compiler_params=params,
    )(
        courant_x, courant_y, diffusion, inner, cells, building, fine_bank, coarse_bank, coarse_code,
        x_even, got_x_even, got_x_odd, y_even,
    )

    def choosing(tiles):
        rows = tiles * NOPS * PB
        return [
            pltpu.VMEM((rows, 2 * CX), BF16),
            pltpu.VMEM((rows, BLK), F32),
        ]

    new, fields, side_fix, side, part_both = pl.pallas_call(
        update_kernel,
        out_shape=(
            shape(VZ, CX, BLK), fields_shape, shape(CX, BLK), shape(2 * CX, BLK, kind=BF16), shape(VZ * PB, BLK),
        ),
        in_specs=[IN_VMEM] * 10,
        out_specs=(IN_VMEM,) * 5,
        input_output_aliases={0: 0, 1: 1},
        scratch_shapes=choosing(1) + [
            pltpu.VMEM((512, V * BLK), BF16),
            pltpu.VMEM((2, VZ * PB, NOPS * BLK), BF16),
        ],
        compiler_params=params,
    )(inner, fields, building, got_y_even, got_y_odd, banks, coarse_banks, counts_y, side_weights, open_sides)
    got_both = one_lower(part_both, "gy")
    part_x, part_y = pl.pallas_call(
        sides_kernel,
        out_shape=(shape(VZ * PB, BLK),) * 2,
        in_specs=[IN_VMEM] * 7,
        out_specs=(IN_VMEM,) * 2,
        scratch_shapes=choosing(2) + [pltpu.VMEM((2, 2 * VZ * PB, NOPS * BLK), BF16)],
        compiler_params=params,
    )(got_x_even, got_x_odd, got_y_even, got_y_odd, fields, side, banks)
    got_x = one_lower(part_x + got_both, "gx")
    got_y = one_lower(part_y, "gy")
    states, comfort, so_far = pl.pallas_call(
        own_kernel,
        out_shape=(shape(VZ, CX, BLK), shape(CX, BLK), shape(VZ * PB, BLK)),
        in_specs=[IN_VMEM] * 8 + [pl.BlockSpec(memory_space=pl.ANY)],
        out_specs=(IN_HBM, IN_VMEM, IN_VMEM),
        scratch_shapes=[pltpu.VMEM((VZ, CX, BLK), F32)] + choosing(1) + [
            pltpu.VMEM((2, VZ * PB, NOPS * BLK), BF16),
            pltpu.SemaphoreType.DMA((V,)),
        ],
        compiler_params=params,
    )(
        x_even, new, side_fix, fields, side, banks, radiative_mean_kelvin, parent_slab.reshape(VZ * PB, BLK), part_y,
    )
    parent_new = so_far + 0.5 * (got_y + got_x)
    return states.reshape(child_state.shape), parent_new.reshape(parent_slab.shape), comfort


def solution(mesh):
    placed = (
        P(None, None, "gx", "gy"),
        P(None, None, ("gx", "gy"), None),
        P(None, ("gx", "gy"), None),
        P("gx", "gy"),
        P(),
        P(),
        P(),
        P(None, "gx", "gy"),
        P(("gx", "gy"), None),
        P(("gx", "gy"), None),
        P(("gx", "gy"), None),
        P(),
        P("gx", "gy", None),
        P("gx", "gy", None),
        P("gx", "gy", None),
        P(),
    )
    return jax.shard_map(
        local,
        mesh=mesh,
        in_specs=placed,
        out_specs=(P(None, None, "gx", "gy"), P(None, None, ("gx", "gy"), None), P("gx", "gy")),
        check_vma=False,
    )
```
